32 devices in a mesh: fsdp: 4 (over z), context: 2 (over x), tensor: 4 (over y, core).
Axes of the slice: x: 2, y: 2, z: 4, core: 2. Of those that a mesh axis runs over, the one named last changes fastest.
Arguments:
- tokens: bfloat16 [2048, 1024], P(('fsdp', 'context')), may hold values from -6 to 6
- w_query: bfloat16 [1024, 1024], P(('fsdp', 'context'), 'tensor'), may hold values from -0.1875 to 0.1875
- key_projection_weight: bfloat16 [1024, 512], P(('fsdp', 'context'), 'tensor'), may hold values from -0.1875 to 0.1875
- value_projection_weight: bfloat16 [1024, 512], P(('fsdp', 'context'), 'tensor'), may hold values from -0.1875 to 0.1875
- w_out: bfloat16 [1024, 1024], P(('fsdp', 'context'), 'tensor'), may hold values from -0.75 to 0.75
- w_gate: bfloat16 [16, 1024, 512], P(None, ('fsdp', 'context'), 'tensor'), may hold values from -0.1875 to 0.1875
- w_up: bfloat16 [16, 1024, 512], P(None, ('fsdp', 'context'), 'tensor'), may hold values from -0.1875 to 0.1875
- w_down: bfloat16 [16, 1024, 512], P(None, ('fsdp', 'context'), 'tensor'), may hold values from -0.25 to 0.25
- norm_in: bfloat16 [1024], P(('fsdp', 'context')), may hold values from 0.5 to 1.5
- norm_mid: bfloat16 [1024], P(('fsdp', 'context')), may hold values from 0.5 to 1.5
- gate_values: float32 [2048, 8], P(('fsdp', 'context')), may hold values from 0.25 to 1
- routes: int32 [2048, 8], P(('fsdp', 'context')), may hold values from 0 to 15, all different within a row; in each aligned block of 256 rows (0 to 255, 256 to 511, ...) at most 144 rows name the same one
- doc_ids: int32 [4, 512], P('fsdp'), may hold values from 0 to 4, as said below
- cotangent: bfloat16 [2048, 1024], P(('fsdp', 'context')), may hold values from -6 to 6
Outputs:
- output: bfloat16 [2048, 1024], P(('fsdp', 'context'))
- d_tokens: bfloat16 [2048, 1024], P(('fsdp', 'context'))
- d_w_query: float32 [1024, 1024], P(('fsdp', 'context'), 'tensor')
- d_w_key: float32 [1024, 512], P(('fsdp', 'context'), 'tensor')
- d_w_value: float32 [1024, 512], P(('fsdp', 'context'), 'tensor')
- d_w_out: float32 [1024, 1024], P(('fsdp', 'context'), 'tensor')
- d_w_gate: float32 [16, 1024, 512], P(None, ('fsdp', 'context'), 'tensor')
- d_w_up: float32 [16, 1024, 512], P(None, ('fsdp', 'context'), 'tensor')
- d_w_down: float32 [16, 1024, 512], P(None, ('fsdp', 'context'), 'tensor')
- d_norm_in: float32 [1024], P(('fsdp', 'context'))
- d_norm_mid: float32 [1024], P(('fsdp', 'context'))
The draws below stay inside these ranges and needn't reach their ends.
Inputs may be any that keep to these rules, and one draw needn't show every extreme that they name: `routes`: in each block of 256 rows (the rows of one device) no expert is named by more than 144 rows; each row names 8 different experts. `doc_ids`: along each group the numbers never fall and begin at 0; the tokens 512/2 - 1 and 256 lie in one document; one group, drawn from the seed, is a single document.
All inputs are finite; a program needn't handle non-finite values.
Results may differ from the reference program's by a relative error of at most 0.013.
Values may be sent and summed in bfloat16 or wider, within the bound.
A program may use at most 128 MiB of HBM per device.

```python
import math
import jax
import jax.numpy as jnp
import numpy as np
from jax import lax

MODEL_DIMENSION = 1024
QUERY_HEADS = 16
KEY_VALUE_HEADS = 8
HEAD_SIZE = 64
FF = 512
TOP = 8
EXPERTS = 16
TOK_DEV = 256
GROUP = 512
TOKENS = 2048
CAP = 144
N_FSDP = 4
N_CONTEXT = 2


def draw_doc_ids(key, part):
    key = jax.random.fold_in(key, 11)
    lower = jax.random.randint(jax.random.fold_in(key, 1), (N_FSDP, 2), 1, GROUP // 2 - GROUP // 8)
    upper = jax.random.randint(jax.random.fold_in(key, 2), (N_FSDP, 2), GROUP // 2 + GROUP // 8, GROUP)
    whole_group = jax.random.randint(jax.random.fold_in(key, 3), (), 0, N_FSDP)
    cuts = jnp.concatenate([lower, upper], axis=1).astype(jnp.int32)
    single = jnp.arange(N_FSDP, dtype=jnp.int32)[:, None] == whole_group
    cuts = jnp.where(single, GROUP, cuts).astype(jnp.int32)
    places = jnp.arange(GROUP, dtype=jnp.int32)
    return jnp.sum((places[None, :, None] >= cuts[:, None, :]).astype(jnp.int32), axis=2).astype(jnp.int32)


def level_of(key, extent, shards, smallest, top_value):
    def one(axis_at, blocks):
        steps = jax.random.uniform(jax.random.fold_in(jax.random.fold_in(key, 6), axis_at), (blocks,), jnp.float32, smallest / len(shards), top_value / len(shards))
        return jnp.repeat(jnp.exp(steps), extent[axis_at] // blocks).reshape((-1,) + (1,) * (len(extent) - axis_at - 1))

    gain = one(*shards[0])
    for cut in shards[1:]:
        gain = gain * one(*cut)
    return gain


def shared_out(key, own, number, rows, count, top, reach, lean):
    order = jax.random.permutation(key, count)
    heavy_load, usual = portions_of(count, rows * top, reach, lean, True), portions_of(count, rows * top, reach, lean, False)
    places = jnp.arange(count)

    def named(tallies, turn):
        used = int((tallies > 0).sum())
        fixed = max(1, used // 4)
        shifted = fixed + (places - fixed + turn * (used - fixed)) % max(1, count - fixed)
        return jnp.zeros((count,), jnp.int32).at[order[jnp.where(places < fixed, places, shifted)]].set(jnp.asarray(tallies, jnp.int32))

    tallies = jnp.where(number % 4 == 0, named(heavy_load, number // 4), named(usual, number - number // 4 - 1))
    mixed = jax.random.permutation(jax.random.fold_in(own, 3), count)
    donor, sink = mixed[0:count // 2 * 2:2], mixed[1:count // 2 * 2:2]
    room = jnp.minimum(tallies[donor] - 1, reach - tallies[sink]) // 2
    room = jnp.where((donor == order[0]) | (sink == order[0]) | (tallies[sink] == 0), 0, jnp.maximum(room, 0))
    shifted = jax.random.randint(jax.random.fold_in(own, 4), (count // 2,), 0, 1 << 20) % (room + 1)
    tallies = tallies.at[donor].add(-shifted).at[sink].add(shifted)
    members = jnp.searchsorted(jnp.cumsum(tallies), jnp.arange(rows * top), side="right").astype(jnp.int32)
    table = members.reshape(top, rows).T
    table = table[jax.random.permutation(jax.random.fold_in(own, 1), rows)]
    turn = jax.random.randint(jax.random.fold_in(own, 2), (rows, 1), 0, top)
    return jnp.take_along_axis(table, (jnp.arange(top)[None, :] + turn) % top, axis=1)


def portions_of(number_of, total, reach, slope, full):
    weights = [(1 << 20) // math.isqrt(rank ** slope) + 1 for rank in range(1, number_of + 1)]
    largest = reach if full else min(reach, max(-(-total // number_of), total * weights[0] // sum(weights)))
    least = 1 if total - largest >= number_of - 1 else 0
    holding, spare = [largest] + [least] * (number_of - 1), total - largest - least * (number_of - 1)
    while spare > 0:
        candidates = [i for i in range(1, number_of) if holding[i] < largest] or [i for i in range(1, number_of) if holding[i] < reach]
        whole, budget = sum([weights[i] for i in candidates]), spare
        for i in candidates:
            extra = min(reach - holding[i], max(1, budget * weights[i] // whole), spare)
            holding[i] = holding[i] + extra
            spare = spare - extra
    return np.array(holding)


def normal_values(own_key, dims, deviation, most, split=(), held_as=jnp.bfloat16):
    level = level_of(own_key, dims, split, -0.22, 0.18) if split else 1.0
    entries = jax.random.normal(own_key, dims, jnp.float32) * deviation * level
    return jnp.minimum(jnp.maximum(entries, -most), most).astype(held_as)


def setup_inputs(seed: int = 0) -> dict:
    splits = jax.random.split(jax.random.key(seed), 15)
    tokens = normal_values(splits[0], (TOKENS, MODEL_DIMENSION), 1.0, 6.0, ((0, 8),))
    w_query = normal_values(splits[1], (MODEL_DIMENSION, QUERY_HEADS * HEAD_SIZE), MODEL_DIMENSION ** -0.5, 0.1875, ((0, 8), (1, 4)))
    key_projection_weight = normal_values(splits[2], (MODEL_DIMENSION, KEY_VALUE_HEADS * HEAD_SIZE), MODEL_DIMENSION ** -0.5, 0.1875, ((0, 8), (1, 4)))
    value_projection_weight = normal_values(splits[3], (MODEL_DIMENSION, KEY_VALUE_HEADS * HEAD_SIZE), MODEL_DIMENSION ** -0.5, 0.1875, ((0, 8), (1, 4)))
    w_out = normal_values(splits[4], (MODEL_DIMENSION, QUERY_HEADS * HEAD_SIZE), (QUERY_HEADS * HEAD_SIZE // 16) ** -0.5, 0.75, ((0, 8), (1, 4)))
    w_gate = normal_values(splits[5], (EXPERTS, MODEL_DIMENSION, FF), MODEL_DIMENSION ** -0.5, 0.1875, ((1, 8), (2, 4)))
    w_up = normal_values(splits[6], (EXPERTS, MODEL_DIMENSION, FF), MODEL_DIMENSION ** -0.5, 0.1875, ((1, 8), (2, 4)))
    w_down = normal_values(splits[7], (EXPERTS, MODEL_DIMENSION, FF), FF ** -0.5, 0.25, ((1, 8), (2, 4)))
    norm_in = jnp.clip(1.0 + 0.1 * jax.random.normal(splits[8], (MODEL_DIMENSION,), jnp.float32), 0.5, 1.5).astype(jnp.bfloat16)
    norm_mid = jnp.clip(1.0 + 0.1 * jax.random.normal(splits[9], (MODEL_DIMENSION,), jnp.float32), 0.5, 1.5).astype(jnp.bfloat16)
    gate_values = jnp.clip(jnp.exp(math.log(1.0) - 1.3862944 * jax.random.uniform(splits[10], (TOKENS, TOP), jnp.float32) ** level_of(splits[10], (TOKENS, TOP), ((0, 8),), -0.2, 0.2)), 0.25, 1.0)
    routes_keys = jax.random.split(jax.random.fold_in(splits[11], 1), TOKENS // TOK_DEV)
    routes_turns = jax.random.permutation(jax.random.fold_in(splits[11], 3), TOKENS // TOK_DEV)
    routes = jax.vmap(lambda own, number: shared_out(jax.random.fold_in(splits[11], 2), own, number, TOK_DEV, EXPERTS, TOP, CAP, 1))(routes_keys, routes_turns).reshape((TOKENS, TOP))
    doc_ids = draw_doc_ids(jax.random.fold_in(splits[14], 71), 0)
    cotangent = normal_values(splits[13], (TOKENS, MODEL_DIMENSION), 1.0, 6.0, ((0, 8),))
    return {"tokens": tokens, "w_query": w_query, "key_projection_weight": key_projection_weight, "value_projection_weight": value_projection_weight, "w_out": w_out, "w_gate": w_gate, "w_up": w_up, "w_down": w_down, "norm_in": norm_in, "norm_mid": norm_mid, "gate_values": gate_values, "routes": routes, "doc_ids": doc_ids, "cotangent": cotangent}


EPSILON = 1e-06
PRECISE = lax.Precision.HIGHEST

@jax.custom_vjp
def low(v):
    return lax.optimization_barrier(v.astype(jnp.bfloat16)).astype(jnp.float32)

@jax.custom_vjp
def low_back(v):
    return v

def low_keep(v):
    return (low(v), None)

def low_pass(kept, grad):
    return (grad,)

def back_keep(v):
    return (v, None)

def back_low(kept, grad):
    return (low(grad),)
low.defvjp(low_keep, low_pass)
low_back.defvjp(back_keep, back_low)

def rms_scale(values):
    return lax.rsqrt(lax.optimization_barrier(jnp.mean(values * values, axis=-1, keepdims=True)) + EPSILON)

def rotate(values, places, direction):
    head_count = values.shape[-1] // HEAD_SIZE
    shaped = values.reshape(values.shape[0], head_count, HEAD_SIZE)
    half_dim = HEAD_SIZE // 2
    frequency = 1.0 / 10000.0 ** (jnp.arange(half_dim, dtype=jnp.float32) * 2.0 / HEAD_SIZE)
    angles = places.astype(jnp.float32)[:, None, None] * frequency[None, None, :]
    cosine = jnp.cos(angles)
    sine_table = jnp.sin(angles) * direction
    first_half = shaped[..., :half_dim]
    second_half = shaped[..., half_dim:]
    turned = jnp.concatenate([first_half * cosine - second_half * sine_table, second_half * cosine + first_half * sine_table], axis=-1)
    return turned.reshape(values.shape)

def slot_table(route_rows):
    flat_routes = route_rows.reshape(-1)
    onehot_table = (flat_routes[:, None] == jnp.arange(EXPERTS, dtype=jnp.int32)[None, :]).astype(jnp.int32)
    earlier = jnp.cumsum(onehot_table, axis=0) - onehot_table
    places = lax.optimization_barrier(jnp.sum(earlier * onehot_table, axis=1))
    slot_ids = (flat_routes * CAP + places).astype(jnp.int32)
    choice_ids = jnp.arange(flat_routes.shape[0], dtype=jnp.int32)
    source = jnp.zeros((EXPERTS * CAP,), jnp.int32).at[slot_ids].set(choice_ids)
    filled = jnp.zeros((EXPERTS * CAP,), jnp.int32).at[slot_ids].set(1) > 0
    return (slot_ids, source, filled)

def expert_block(normed, gate_rows, route_rows, w_gate, w_up, w_down):
    slot_ids, source, filled = slot_table(route_rows)
    gathered_rows = jnp.where(filled[:, None], normed[source // TOP], 0.0)
    expert_in = gathered_rows.reshape(EXPERTS, CAP, normed.shape[1])
    gate_act = low_back(jnp.einsum('ecd,edf->ecf', expert_in, w_gate, precision=PRECISE))
    up_act = low_back(jnp.einsum('ecd,edf->ecf', expert_in, w_up, precision=PRECISE))
    hidden = low(gate_act * jax.nn.sigmoid(gate_act) * up_act)
    expert_out = low_back(jnp.einsum('ecf,edf->ecd', hidden, w_down, precision=PRECISE))
    expert_out = expert_out.reshape(EXPERTS * CAP, normed.shape[1])
    picked = expert_out[slot_ids].reshape(gate_rows.shape[0], TOP, normed.shape[1])
    return lax.optimization_barrier(jnp.sum(gate_rows[:, :, None] * picked, axis=1))

def group_forward(params, tokens_group, docs_group, gates_group, routes_group):
    w_query, key_projection_weight, value_projection_weight, w_out, w_gate, w_up, w_down, norm_in, norm_mid = params
    sequence_length = tokens_group.shape[0]
    normed_in = low(tokens_group * rms_scale(tokens_group) * norm_in)
    places = jnp.arange(sequence_length, dtype=jnp.int32)
    query_raw = low_back(jnp.dot(normed_in, w_query, precision=PRECISE))
    key_raw = low_back(jnp.dot(normed_in, key_projection_weight, precision=PRECISE))
    value_input = low(low_back(jnp.dot(normed_in, value_projection_weight, precision=PRECISE)))
    query_input = low(rotate(query_raw, places, 1.0))
    key_input = low(rotate(key_raw, places, 1.0))
    query_head_rows = query_input.reshape(sequence_length, KEY_VALUE_HEADS, QUERY_HEADS // KEY_VALUE_HEADS, HEAD_SIZE)
    key_head_rows = key_input.reshape(sequence_length, KEY_VALUE_HEADS, HEAD_SIZE)
    value_head_rows = value_input.reshape(sequence_length, KEY_VALUE_HEADS, HEAD_SIZE)
    scores = low_back(HEAD_SIZE ** (-0.5) * jnp.einsum('rkgd,skd->kgrs', query_head_rows, key_head_rows, precision=PRECISE))
    visible = (places[None, :] <= places[:, None]) & (docs_group[None, :] == docs_group[:, None])
    masked = jnp.where(visible, scores, -1e+30)
    highest = lax.optimization_barrier(jnp.max(masked, axis=-1, keepdims=True))
    exponent = jnp.exp(masked - highest)
    probs = exponent / lax.optimization_barrier(jnp.sum(exponent, axis=-1, keepdims=True))
    probs_low = low(probs)
    context = jnp.einsum('kgrs,skd->rkgd', probs_low, value_head_rows, precision=PRECISE).reshape(sequence_length, QUERY_HEADS * HEAD_SIZE)
    context = low(low_back(context))
    attended = low_back(jnp.dot(context, w_out.T, precision=PRECISE))
    hidden_state = tokens_group + attended
    normed_mid = low(hidden_state * rms_scale(hidden_state) * norm_mid)
    pieces = []
    for block in range(N_CONTEXT):
        lower = block * TOK_DEV
        upper = lower + TOK_DEV
        pieces.append(expert_block(normed_mid[lower:upper], gates_group[lower:upper], routes_group[lower:upper], w_gate, w_up, w_down))
    return hidden_state + jnp.concatenate(pieces, axis=0)

def reference(tokens, w_query, key_projection_weight, value_projection_weight, w_out, w_gate, w_up, w_down, norm_in, norm_mid, gate_values, routes, doc_ids, cotangent):
    inputs = tokens.astype(jnp.float32)
    weight_list = (w_query, key_projection_weight, value_projection_weight, w_out, w_gate, w_up, w_down, norm_in, norm_mid)
    weight_list = tuple((array.astype(jnp.float32) for array in weight_list))

    def forward(block_input, *params):

        def group_step(carried, pieces):
            return (carried, group_forward(params, pieces[0], pieces[1], pieces[2], pieces[3]))
        pieces = (block_input.reshape(N_FSDP, GROUP, MODEL_DIMENSION), doc_ids, gate_values.reshape(N_FSDP, GROUP, TOP), routes.reshape(N_FSDP, GROUP, TOP))
        carried, outputs = lax.scan(group_step, jnp.zeros((), jnp.float32), pieces)
        return outputs.reshape(TOKENS, MODEL_DIMENSION)
    result, pullback = jax.vjp(forward, inputs, *weight_list)
    gradients = pullback(cotangent.astype(jnp.float32))
    return (result.astype(jnp.bfloat16), gradients[0].astype(jnp.bfloat16), gradients[1], gradients[2], gradients[3], gradients[4], gradients[5], gradients[6], gradients[7], gradients[8], gradients[9])
```

```python
import functools

import jax
import jax.numpy as jnp
from jax import lax
from jax.experimental import pallas as pl
from jax.experimental.pallas import tpu as pltpu
from jax.sharding import PartitionSpec as P

HEAD_SIZE = 64
TOP = 8
EXPERTS = 16

EPSILON = 1e-06
CONTRACT_ROWS = (((0,), (0,)), ((), ()))
CONTRACT_COLUMNS = (((1,), (1,)), ((), ()))
MESH = pl.DeviceIdType.MESH
VMEM_BYTES = 48 * 1024 * 1024


def coordinate(dim):
    axis, size, stride = dim
    return lax.rem(lax.div(lax.axis_index(axis), stride), size)


def device_at(dim, place):
    axis, _, stride = dim
    return {axis: lax.axis_index(axis) + (place - coordinate(dim)) * stride}


def greet(dims):
    barrier = pltpu.get_barrier_semaphore()
    total = 0
    for dim in dims:
        for k in range(1, dim[1]):
            place = lax.rem(coordinate(dim) + k, dim[1])
            pl.semaphore_signal(
                barrier, inc=1, device_id=device_at(dim, place), device_id_type=MESH
            )
            total += 1
    pl.semaphore_wait(barrier, total)


def gather_kernel(dims, count, *refs):
    sources, outs = refs[:count], refs[count : 2 * count]
    send_sem, recv_sem, own_sem = refs[2 * count :]
    places = [coordinate(dim) for dim in dims]

    def slot(steps):
        return tuple(
            lax.rem(place - step + dim[1], dim[1]) for place, step, dim in zip(places, steps, dims)
        )

    zero = (0,) * len(dims)
    own = [
        pltpu.make_async_copy(sources[a], outs[a].at[slot(zero)], own_sem.at[a])
        for a in range(count)
    ]
    for copy in own:
        copy.start()
    greet(dims)
    queue = [(zero, 0, None)]
    sent = []
    at = 0
    while at < len(queue):
        steps, level, arriving = queue[at]
        at += 1
        if arriving is not None:
            for copy in arriving:
                copy.wait_recv()
        for s in range(level, len(dims)):
            for k in range(1, dims[s][1]):
                copies = []
                for a in range(count):
                    index = len(sent)
                    source = sources[a] if arriving is None else outs[a].at[slot(steps)]
                    copy = pltpu.make_async_remote_copy(
                        src_ref=source,
                        dst_ref=outs[a].at[slot(steps)],
                        send_sem=send_sem.at[index],
                        recv_sem=recv_sem.at[index],
                        device_id=device_at(dims[s], lax.rem(places[s] + k, dims[s][1])),
                        device_id_type=MESH,
                    )
                    copy.start()
                    copies.append(copy)
                    sent.append(copy)
                queue.append((steps[:s] + (k,) + steps[s + 1 :], s + 1, copies))
    for copy in sent:
        copy.wait_send()
    for copy in own:
        copy.wait()


def gather_pieces(arrays, dims, number):
    sizes = tuple(dim[1] for dim in dims)
    total = 1
    for size in sizes:
        total *= size
    copies = (total - 1) * len(arrays)
    any_spec = pl.BlockSpec(memory_space=pl.ANY)
    return pl.pallas_call(
        functools.partial(gather_kernel, dims, len(arrays)),
        out_shape=tuple(jax.ShapeDtypeStruct(sizes + a.shape, a.dtype) for a in arrays),
        in_specs=[any_spec] * len(arrays),
        out_specs=tuple(any_spec for _ in arrays),
        scratch_shapes=[
            pltpu.SemaphoreType.DMA((max(copies, 1),)),
            pltpu.SemaphoreType.DMA((max(copies, 1),)),
            pltpu.SemaphoreType.DMA((len(arrays),)),
        ],
        compiler_params=pltpu.CompilerParams(collective_id=number, has_side_effects=True),
    )(*arrays)


def reduce_kernel(halves, last, x_ref, out_ref, *scratch):
    stages = len(halves)
    landed = scratch[:stages]
    summed = scratch[stages : 2 * stages]
    final = scratch[2 * stages]
    send_sem, recv_sem = scratch[2 * stages + 1 :]
    n = last[1]
    place = coordinate(last)
    mine = [coordinate(dim) for dim in halves]
    greet(list(halves) + [last])
    order = [lax.rem(place + k, n) for k in list(range(1, n)) + [0]]

    def held(stage):
        return x_ref if stage == 0 else summed[stage - 1]

    def part(stage, j, which):
        return (j,) + (slice(None),) * (stages - 1 - stage) + (which,)

    copies = [[None] * n for _ in range(stages)]

    def push(stage, i):
        copies[stage][i] = pltpu.make_async_remote_copy(
            src_ref=held(stage).at[part(stage, order[i], 1 - mine[stage])],
            dst_ref=landed[stage].at[i],
            send_sem=send_sem.at[stage * n + i],
            recv_sem=recv_sem.at[stage * n + i],
            device_id=device_at(halves[stage], 1 - mine[stage]),
            device_id_type=MESH,
        )
        copies[stage][i].start()

    def merge(stage, i):
        copies[stage][i].wait_recv()
        kept = held(stage)[part(stage, order[i], mine[stage])]
        both = kept.astype(jnp.float32) + landed[stage][i].astype(jnp.float32)
        summed[stage][order[i]] = both.astype(summed[stage].dtype)

    for i in range(n):
        push(0, i)
    outgoing = []
    for tick in range(n + stages - 1):
        for stage in range(stages):
            i = tick - stage
            if 0 <= i < n:
                merge(stage, i)
                if stage + 1 < stages:
                    push(stage + 1, i)
                elif i < n - 1:
                    index = stages * n + i
                    copy = pltpu.make_async_remote_copy(
                        src_ref=summed[-1].at[order[i]],
                        dst_ref=final.at[i],
                        send_sem=send_sem.at[index],
                        recv_sem=recv_sem.at[index],
                        device_id=device_at(last, order[i]),
                        device_id_type=MESH,
                    )
                    copy.start()
                    outgoing.append(copy)
    total = summed[-1][place].astype(jnp.float32)
    for i, copy in enumerate(outgoing):
        copy.wait_recv()
        total = total + final[i].astype(jnp.float32)
    out_ref[...] = total
    for row in copies:
        for copy in row:
            copy.wait_send()
    for copy in outgoing:
        copy.wait_send()


def reduce_pieces(x, halves, last, number):
    rows, columns = x.shape[-2:]
    n = last[1]
    stages = len(halves)
    shapes = [(n,) + (2,) * (stages - 1 - s) + (rows, columns) for s in range(stages)]
    vmem = pl.BlockSpec(memory_space=pltpu.VMEM)
    return pl.pallas_call(
        functools.partial(reduce_kernel, tuple(halves), last),
        out_shape=jax.ShapeDtypeStruct((rows, columns), jnp.float32),
        in_specs=[vmem],
        out_specs=vmem,
        scratch_shapes=[pltpu.VMEM(shape, x.dtype) for shape in shapes]
        + [pltpu.VMEM(shape, x.dtype) for shape in shapes]
        + [
            pltpu.VMEM((n - 1, rows, columns), x.dtype),
            pltpu.SemaphoreType.DMA(((stages + 1) * n,)),
            pltpu.SemaphoreType.DMA(((stages + 1) * n,)),
        ],
        compiler_params=pltpu.CompilerParams(
            collective_id=number, has_side_effects=True, vmem_limit_bytes=VMEM_BYTES
        ),
    )(x)


def swapped(array, axis, step):
    size = lax.axis_size(axis)
    return lax.ppermute(array, axis, [(i, i ^ step) for i in range(size)])


def joined(array, other, place):
    return jnp.where(place == 0, jnp.stack([array, other]), jnp.stack([other, array]))


def by_fsdp(array, dim):
    axis, size, stride = dim
    count = lax.axis_size(axis)
    place = coordinate(dim)
    blocks = [array]
    for k in range(1, size):
        pairs = []
        for i in range(count):
            c = i // stride % size
            pairs.append((i, i + ((c - k) % size - c) * stride))
        blocks.append(lax.ppermute(array, axis, pairs))
    stacked = jnp.stack(blocks)
    order = lax.rem(jnp.arange(size, dtype=jnp.int32) - place + size, size)
    return stacked[order]


def rms_scale(values):
    return lax.rsqrt(jnp.mean(values * values, axis=-1, keepdims=True) + EPSILON)


def rotate(values, places, direction):
    head_count = values.shape[-1] // HEAD_SIZE
    shaped = values.reshape(values.shape[0], head_count, HEAD_SIZE)
    half_dim = HEAD_SIZE // 2
    frequency = 1.0 / 10000.0 ** (jnp.arange(half_dim, dtype=jnp.float32) * 2.0 / HEAD_SIZE)
    angles = places.astype(jnp.float32)[:, None, None] * frequency[None, None, :]
    cosine = jnp.cos(angles)
    sine_table = jnp.sin(angles) * direction
    first_half = shaped[..., :half_dim]
    second_half = shaped[..., half_dim:]
    turned = jnp.concatenate(
        [
            first_half * cosine - second_half * sine_table,
            second_half * cosine + first_half * sine_table,
        ],
        axis=-1,
    )
    return turned.reshape(values.shape)


def local(
    tokens,
    w_query,
    key_projection_weight,
    value_projection_weight,
    w_out,
    w_gate,
    w_up,
    w_down,
    norm_in,
    norm_mid,
    gate_values,
    routes,
    doc_ids,
    cotangent,
):
    local_rows, model_width = tokens.shape
    fsdp = lax.axis_size("fsdp")
    tensor = lax.axis_size("tensor")
    groups = min(fsdp, EXPERTS)
    copies = fsdp // groups
    per_owner = EXPERTS // groups
    piece = local_rows // tensor
    depth = w_gate.shape[1]
    hidden_width = w_gate.shape[2]
    context_index = lax.axis_index("context")
    tensor_index = lax.axis_index("tensor")
    fsdp_all = ("fsdp", fsdp, 1)
    fsdp_dim = ("fsdp", groups, copies)
    context_dim = ("context", lax.axis_size("context"), 1)
    core_dim = ("tensor", 2, 1)
    y_dim = ("tensor", tensor // 2, 2)
    q_width, k_width = w_query.shape[1], key_projection_weight.shape[1]
    columns = per_owner * hidden_width

    def to_owner(weight):
        blocks = jnp.transpose(weight.reshape(groups, per_owner, depth, hidden_width), (0, 2, 1, 3))
        return blocks.reshape(groups, depth, columns)

    packed = jnp.concatenate([to_owner(w_gate), to_owner(w_up), to_owner(w_down)], axis=2)
    packed = jnp.repeat(packed, copies, axis=0)
    from_fsdp = lax.all_to_all(packed, "fsdp", 0, 0, tiled=True)
    both_context = joined(from_fsdp, swapped(from_fsdp, "context", 1), context_index)
    expert_weight = jnp.swapaxes(both_context, 0, 1).reshape(model_width, 3 * columns)
    gate_up_weight = expert_weight[:, : 2 * columns]
    down_weight = expert_weight[:, 2 * columns :]

    cot_piece = lax.dynamic_slice_in_dim(cotangent, tensor_index * piece, piece, 0)
    cot_f = by_fsdp(cot_piece, fsdp_dim)
    cot_y = by_fsdp(cot_f, y_dim)
    cot_t = by_fsdp(cot_y, core_dim)
    cot_all = jnp.transpose(cot_t, (2, 1, 0, 3, 4)).reshape(-1, model_width)
    dense_gates = jnp.sum(
        jnp.where(
            routes.T[None, :, :] == jnp.arange(EXPERTS, dtype=jnp.int32)[:, None, None],
            gate_values.T[None, :, :],
            0.0,
        ),
        axis=1,
    )
    gates_all = by_fsdp(dense_gates, fsdp_dim)
    gates_own = lax.dynamic_slice_in_dim(
        gates_all, coordinate(fsdp_dim) * per_owner, per_owner, 1
    )
    gates_rows = jnp.transpose(gates_own, (0, 2, 1)).reshape(-1, per_owner)
    gates_wide = jnp.repeat(gates_rows, hidden_width, axis=1)

    attn_shard = jnp.concatenate(
        [w_query, key_projection_weight, value_projection_weight, w_out], axis=1
    )
    gain_shard = jnp.pad(
        jnp.stack([norm_in, norm_mid]).astype(jnp.float32), ((0, 6), (0, 128 - depth))
    )
    attn_weight, gains = gather_pieces([attn_shard, gain_shard], [fsdp_all, context_dim], 1)
    attn_weight = attn_weight.reshape(model_width, -1)
    gains = gains[..., :depth].reshape(-1, 8, depth)
    gain_one = gains[:, 0, :].reshape(-1)
    gain_two = gains[:, 1, :].reshape(-1)
    in_weight = attn_weight[:, : q_width + 2 * k_width]
    out_weight = attn_weight[:, q_width + 2 * k_width :]
    documents = doc_ids[0]
    query_places = context_index * local_rows + jnp.arange(local_rows, dtype=jnp.int32)
    key_places = jnp.arange(documents.shape[0], dtype=jnp.int32)
    score_scale = HEAD_SIZE ** (-0.5)
    inputs = tokens.astype(jnp.float32)
    scale_in = rms_scale(inputs)
    normed_in = (inputs * scale_in * gain_one).astype(jnp.bfloat16)
    projected = jnp.dot(normed_in, in_weight, preferred_element_type=jnp.float32)
    query_input = rotate(projected[:, :q_width], query_places, 1.0).astype(jnp.bfloat16)
    key_local = rotate(projected[:, q_width : q_width + k_width], query_places, 1.0)
    key_value = jnp.concatenate([key_local, projected[:, q_width + k_width :]], axis=1).astype(
        jnp.bfloat16
    )
    key_value = joined(key_value, swapped(key_value, "context", 1), context_index).reshape(
        -1, 2 * k_width
    )
    keys_all, values_all = key_value[:, :k_width], key_value[:, k_width:]
    kv_heads = keys_all.shape[1] // HEAD_SIZE
    per_group = query_input.shape[1] // HEAD_SIZE // kv_heads
    query_head_rows = query_input.reshape(local_rows, kv_heads, per_group, HEAD_SIZE)
    key_head_rows = keys_all.reshape(keys_all.shape[0], kv_heads, HEAD_SIZE)
    value_head_rows = values_all.reshape(values_all.shape[0], kv_heads, HEAD_SIZE)
    visible = (key_places[None, :] <= query_places[:, None]) & (
        documents[None, :] == documents[query_places][:, None]
    )

    def masked_scores():
        raw_scores = (
            jnp.einsum(
                "rkgd,skd->kgrs", query_head_rows, key_head_rows, preferred_element_type=jnp.float32
            )
            * score_scale
        )
        return jnp.where(visible, raw_scores, -1e30)

    masked = masked_scores()
    highest = jnp.max(masked, axis=-1, keepdims=True)
    exponent = jnp.exp(masked - highest)
    totals = jnp.sum(exponent, axis=-1, keepdims=True)
    probs_low = (exponent / totals).astype(jnp.bfloat16)
    context = jnp.einsum(
        "kgrs,skd->rkgd", probs_low, value_head_rows, preferred_element_type=jnp.float32
    )
    context = context.reshape(local_rows, -1).astype(jnp.bfloat16)
    attn_part = lax.dot_general(
        context, out_weight, CONTRACT_COLUMNS, preferred_element_type=jnp.float32
    )
    def by_tensor(part):
        return part.astype(jnp.bfloat16).reshape(tensor // 2, 2, piece, model_width)

    attended = reduce_pieces(by_tensor(attn_part), [core_dim], y_dim, 2)
    start_row = tensor_index * piece
    own_inputs = lax.dynamic_slice_in_dim(tokens, start_row, piece, 0).astype(jnp.float32)
    own_scale_in = lax.dynamic_slice_in_dim(scale_in, start_row, piece, 0)
    hidden_state = own_inputs + attended
    scale_mid = rms_scale(hidden_state)
    normed_mid = (hidden_state * scale_mid * gain_two).astype(jnp.bfloat16)
    (expert_rows,) = gather_pieces([normed_mid], [fsdp_dim, y_dim, core_dim], 3)
    expert_rows = expert_rows.reshape(-1, model_width)
    act = jnp.dot(expert_rows, gate_up_weight, preferred_element_type=jnp.float32)
    gate_act, up_act = act[:, :columns], act[:, columns:]
    sigmoid_gate = jax.nn.sigmoid(gate_act)
    swish_act = gate_act * sigmoid_gate
    hidden = (gates_wide * swish_act * up_act).astype(jnp.bfloat16)
    d_hidden = gates_wide * jnp.dot(cot_all, down_weight, preferred_element_type=jnp.float32)
    d_gate_act = d_hidden * up_act * sigmoid_gate * (1.0 + gate_act * (1.0 - sigmoid_gate))
    d_up_act = d_hidden * swish_act
    d_act = jnp.concatenate([d_gate_act, d_up_act], axis=1).astype(jnp.bfloat16)
    moe_part = lax.dot_general(
        hidden, down_weight, CONTRACT_COLUMNS, preferred_element_type=jnp.float32
    ).astype(jnp.bfloat16)
    d_mid_part = lax.dot_general(
        d_act, gate_up_weight, CONTRACT_COLUMNS, preferred_element_type=jnp.float32
    ).astype(jnp.bfloat16)
    split = (groups, tensor // 2, 2, piece, model_width)
    both_parts = jnp.concatenate([moe_part.reshape(split), d_mid_part.reshape(split)], axis=3)
    back = reduce_pieces(both_parts, [core_dim, y_dim], fsdp_dim, 4)
    grad_gate_up = lax.dot_general(
        expert_rows, d_act, CONTRACT_ROWS, preferred_element_type=jnp.float32
    )
    grad_down = lax.dot_general(cot_all, hidden, CONTRACT_ROWS, preferred_element_type=jnp.float32)
    expert_grad = jnp.concatenate([grad_gate_up, grad_down], axis=1).astype(jnp.bfloat16)
    expert_grad = jnp.swapaxes(expert_grad.reshape(fsdp, -1, depth, 3 * columns), 0, 1)
    kept = lax.dynamic_index_in_dim(expert_grad, context_index, 0, False)
    given = lax.dynamic_index_in_dim(expert_grad, 1 - context_index, 0, False)
    taken = swapped(given, "context", 1)
    half_grad = (kept.astype(jnp.float32) + taken.astype(jnp.float32)).astype(jnp.bfloat16)
    owned_grad = lax.all_to_all(half_grad, "fsdp", 0, 0, tiled=True).astype(jnp.float32)
    owned_grad = jnp.sum(owned_grad.reshape(groups, copies, depth, 3, per_owner, hidden_width), 1)
    owned_grad = jnp.transpose(owned_grad, (2, 0, 3, 1, 4)).reshape(
        3, EXPERTS, depth, hidden_width
    )

    moe_mixed, d_mid = back[:piece], back[piece:]
    own_output = (hidden_state + moe_mixed).astype(jnp.bfloat16)
    d_gain_mid = jnp.sum(d_mid * hidden_state * scale_mid, axis=0)
    d_hidden_state = (
        cot_piece.astype(jnp.float32)
        + d_mid * gain_two * scale_mid
        - hidden_state
        * scale_mid**3
        * jnp.mean(gain_two * d_mid * hidden_state, axis=-1, keepdims=True)
    )
    d_attended, output = gather_pieces(
        [d_hidden_state.astype(jnp.bfloat16), own_output], [y_dim, core_dim], 5
    )
    d_attended = d_attended.reshape(local_rows, model_width)
    output = output.reshape(local_rows, model_width)
    d_out_weight = lax.dot_general(
        d_attended, context, CONTRACT_ROWS, preferred_element_type=jnp.float32
    )
    d_context = jnp.dot(d_attended, out_weight, preferred_element_type=jnp.float32).astype(
        jnp.bfloat16
    )
    d_context_heads = d_context.reshape(local_rows, kv_heads, per_group, HEAD_SIZE)
    attn_probs = jnp.exp(masked_scores() - highest) / totals
    d_probs = jnp.einsum(
        "rkgd,skd->kgrs", d_context_heads, value_head_rows, preferred_element_type=jnp.float32
    )
    d_scores = attn_probs * (d_probs - jnp.sum(attn_probs * d_probs, axis=-1, keepdims=True))
    d_scores_low = jnp.where(visible, d_scores, 0.0).astype(jnp.bfloat16)
    d_query_turned = jnp.einsum(
        "kgrs,skd->rkgd", d_scores_low, key_head_rows, preferred_element_type=jnp.float32
    )
    d_query_turned = d_query_turned.reshape(local_rows, -1) * score_scale
    d_keys = jnp.einsum(
        "kgrs,rkgd->skd", d_scores_low, query_head_rows, preferred_element_type=jnp.float32
    )
    d_keys = d_keys.reshape(keys_all.shape[0], -1) * score_scale
    d_values = jnp.einsum(
        "kgrs,rkgd->skd", probs_low, d_context_heads, preferred_element_type=jnp.float32
    )
    d_values = d_values.reshape(values_all.shape[0], -1)
    d_both = jnp.concatenate([d_keys, d_values], axis=1).reshape(
        -1, local_rows, 2 * k_width
    )
    d_given = lax.dynamic_index_in_dim(d_both, 1 - context_index, 0, False)
    d_kept = lax.dynamic_index_in_dim(d_both, context_index, 0, False)
    d_own = d_kept + swapped(d_given, "context", 1)
    d_query = rotate(d_query_turned, query_places, -1.0).astype(jnp.bfloat16)
    d_key = rotate(d_own[:, :k_width], query_places, -1.0).astype(jnp.bfloat16)
    d_projected = jnp.concatenate(
        [d_query, d_key, d_own[:, k_width:].astype(jnp.bfloat16)], axis=1
    )
    d_in_part = lax.dot_general(
        d_projected, in_weight, CONTRACT_COLUMNS, preferred_element_type=jnp.float32
    )
    d_in = reduce_pieces(by_tensor(d_in_part), [core_dim], y_dim, 6)
    d_in_weight = lax.dot_general(
        normed_in, d_projected, CONTRACT_ROWS, preferred_element_type=jnp.float32
    )
    d_gain_in = jnp.sum(d_in * own_inputs * own_scale_in, axis=0)
    d_inputs = (
        d_hidden_state
        + d_in * gain_one * own_scale_in
        - own_inputs
        * own_scale_in**3
        * jnp.mean(gain_one * d_in * own_inputs, axis=-1, keepdims=True)
    ).astype(jnp.bfloat16)
    d_gains = jnp.pad(jnp.stack([d_gain_in, d_gain_mid]), ((0, 6), (0, 0)))
    d_tokens, d_gains = gather_pieces([d_inputs, d_gains], [y_dim, core_dim], 7)
    d_tokens = d_tokens.reshape(local_rows, model_width)
    d_gains = jnp.sum(d_gains, axis=(0, 1))[:2]
    d_attn = jnp.concatenate([d_in_weight, d_out_weight], axis=1).astype(jnp.bfloat16)
    d_attn = d_attn.reshape(fsdp, -1, depth, d_attn.shape[1])
    d_gains = jnp.transpose(d_gains.reshape(2, fsdp, -1, depth), (1, 2, 0, 3)).astype(jnp.bfloat16)
    d_gains = jnp.pad(d_gains, ((0, 0), (0, 0), (0, 14), (0, d_attn.shape[3] - depth)))
    owned = reduce_pieces(
        jnp.concatenate([d_attn, d_gains], axis=2), [context_dim], fsdp_all, 8
    )
    first, second = q_width, q_width + k_width
    third = q_width + 2 * k_width
    return (
        output,
        d_tokens,
        owned[:depth, :first],
        owned[:depth, first:second],
        owned[:depth, second:third],
        owned[:depth, third:],
        owned_grad[0],
        owned_grad[1],
        owned_grad[2],
        owned[depth, :depth],
        owned[depth + 1, :depth],
    )


def solution(mesh):
    placed = (
        P(("fsdp", "context"), None),
        P(("fsdp", "context"), "tensor"),
        P(("fsdp", "context"), "tensor"),
        P(("fsdp", "context"), "tensor"),
        P(("fsdp", "context"), "tensor"),
        P(None, ("fsdp", "context"), "tensor"),
        P(None, ("fsdp", "context"), "tensor"),
        P(None, ("fsdp", "context"), "tensor"),
        P(("fsdp", "context")),
        P(("fsdp", "context")),
        P(("fsdp", "context"), None),
        P(("fsdp", "context"), None),
        P("fsdp", None),
        P(("fsdp", "context"), None),
    )
    return jax.shard_map(
        local,
        mesh=mesh,
        in_specs=placed,
        out_specs=(
            P(("fsdp", "context"), None),
            P(("fsdp", "context"), None),
            P(("fsdp", "context"), "tensor"),
            P(("fsdp", "context"), "tensor"),
            P(("fsdp", "context"), "tensor"),
            P(("fsdp", "context"), "tensor"),
            P(None, ("fsdp", "context"), "tensor"),
            P(None, ("fsdp", "context"), "tensor"),
            P(None, ("fsdp", "context"), "tensor"),
            P(("fsdp", "context")),
            P(("fsdp", "context")),
        ),
        check_vma=False,
    )
```

```python
import functools
import math

import jax
import jax.numpy as jnp
from jax import lax
from jax.experimental import pallas as pl
from jax.experimental.pallas import tpu as pltpu
from jax.sharding import PartitionSpec as P

HEAD_SIZE = 64
TOP = 8
EXPERTS = 16

EPSILON = 1e-06
CONTRACT_ROWS = (((0,), (0,)), ((), ()))
CONTRACT_COLUMNS = (((1,), (1,)), ((), ()))
MESH = pl.DeviceIdType.MESH
VMEM_BYTES = 48 * 1024 * 1024


def coordinate(dim):
    axis, size, stride = dim
    return lax.rem(lax.div(lax.axis_index(axis), stride), size)


def device_at(dim, place):
    axis, _, stride = dim
    return {axis: lax.axis_index(axis) + (place - coordinate(dim)) * stride}


def greet(dims):
    barrier = pltpu.get_barrier_semaphore()
    total = 0
    for dim in dims:
        for k in range(1, dim[1]):
            place = lax.rem(coordinate(dim) + k, dim[1])
            pl.semaphore_signal(
                barrier, inc=1, device_id=device_at(dim, place), device_id_type=MESH
            )
            total += 1
    pl.semaphore_wait(barrier, total)


def gather_kernel(jobs, *refs):
    count = len(jobs)
    sources, outs = refs[:count], refs[count : 2 * count]
    send_sem, recv_sem, own_sem = refs[2 * count :]

    def slot(dims, steps):
        return tuple(
            lax.rem(coordinate(dim) - step + dim[1], dim[1]) for step, dim in zip(steps, dims)
        )

    own = []
    for a, dims in enumerate(jobs):
        at = slot(dims, (0,) * len(dims))
        own.append(pltpu.make_async_copy(sources[a], outs[a].at[at], own_sem.at[a]))
    greet(unique(dim for dims in jobs for dim in dims))
    sent = []
    queues = [[] for _ in jobs]

    def forward(a, steps, level, source):
        dims = jobs[a]
        for s in range(level, len(dims)):
            for k in range(1, dims[s][1]):
                index = len(sent)
                copy = pltpu.make_async_remote_copy(
                    src_ref=source,
                    dst_ref=outs[a].at[slot(dims, steps)],
                    send_sem=send_sem.at[index],
                    recv_sem=recv_sem.at[index],
                    device_id=device_at(dims[s], lax.rem(coordinate(dims[s]) + k, dims[s][1])),
                    device_id_type=MESH,
                )
                copy.start()
                sent.append(copy)
                queues[a].append((steps[:s] + (k,) + steps[s + 1 :], s + 1, copy))

    for a, dims in enumerate(jobs):
        forward(a, (0,) * len(dims), 0, sources[a])
    for copy in own:
        copy.start()
    for a, dims in enumerate(jobs):
        at = 0
        while at < len(queues[a]):
            steps, level, copy = queues[a][at]
            at += 1
            copy.wait_recv()
            forward(a, steps, level, outs[a].at[slot(dims, steps)])
    for copy in sent:
        copy.wait_send()
    for copy in own:
        copy.wait()


def unique(dims):
    kept = []
    for dim in dims:
        if dim not in kept:
            kept.append(dim)
    return kept


def gather_pieces(arrays, jobs, number):
    shapes, copies = [], 0
    for a, dims in zip(arrays, jobs):
        sizes = tuple(dim[1] for dim in dims)
        shapes.append(jax.ShapeDtypeStruct(sizes + a.shape, a.dtype))
        copies += math.prod(sizes) - 1
    any_spec = pl.BlockSpec(memory_space=pl.ANY)
    return pl.pallas_call(
        functools.partial(gather_kernel, jobs),
        out_shape=tuple(shapes),
        in_specs=[any_spec] * len(arrays),
        out_specs=tuple(any_spec for _ in arrays),
        scratch_shapes=[
            pltpu.SemaphoreType.DMA((copies,)),
            pltpu.SemaphoreType.DMA((copies,)),
            pltpu.SemaphoreType.DMA((len(arrays),)),
        ],
        compiler_params=pltpu.CompilerParams(collective_id=number, has_side_effects=True),
    )(*arrays)


def reduce_kernel(halves, last, side, *refs):
    if side is None:
        x_ref, out_ref, *scratch = refs
    else:
        x_ref, given_ref, out_ref, taken_ref, *scratch, side_send, side_recv = refs
    stages = len(halves)
    landed = scratch[:stages]
    summed = scratch[stages : 2 * stages]
    final = scratch[2 * stages]
    send_sem, recv_sem = scratch[2 * stages + 1 :]
    n = last[1]
    place = coordinate(last)
    mine = [coordinate(dim) for dim in halves]
    greet(list(halves) + [last] + ([] if side is None else [side]))
    order = [lax.rem(place + k, n) for k in list(range(1, n)) + [0]]

    def held(stage):
        return x_ref if stage == 0 else summed[stage - 1]

    def part(stage, j, which):
        return (j,) + (slice(None),) * (stages - 1 - stage) + (which,)

    copies = [[None] * n for _ in range(stages)]

    def push(stage, i):
        copies[stage][i] = pltpu.make_async_remote_copy(
            src_ref=held(stage).at[part(stage, order[i], 1 - mine[stage])],
            dst_ref=landed[stage].at[i],
            send_sem=send_sem.at[stage * n + i],
            recv_sem=recv_sem.at[stage * n + i],
            device_id=device_at(halves[stage], 1 - mine[stage]),
            device_id_type=MESH,
        )
        copies[stage][i].start()

    def merge(stage, i):
        copies[stage][i].wait_recv()
        kept = held(stage)[part(stage, order[i], mine[stage])]
        both = kept.astype(jnp.float32) + landed[stage][i].astype(jnp.float32)
        summed[stage][order[i]] = both.astype(summed[stage].dtype)

    for i in range(n):
        push(0, i)
    if side is not None:
        exchange = pltpu.make_async_remote_copy(
            src_ref=given_ref.at[1 - coordinate(side)],
            dst_ref=taken_ref,
            send_sem=side_send,
            recv_sem=side_recv,
            device_id=device_at(side, 1 - coordinate(side)),
            device_id_type=MESH,
        )
        exchange.start()
    outgoing = []
    for tick in range(n + stages - 1):
        for stage in range(stages):
            i = tick - stage
            if 0 <= i < n:
                merge(stage, i)
                if stage + 1 < stages:
                    push(stage + 1, i)
                elif i < n - 1:
                    index = stages * n + i
                    copy = pltpu.make_async_remote_copy(
                        src_ref=summed[-1].at[order[i]],
                        dst_ref=final.at[i],
                        send_sem=send_sem.at[index],
                        recv_sem=recv_sem.at[index],
                        device_id=device_at(last, order[i]),
                        device_id_type=MESH,
                    )
                    copy.start()
                    outgoing.append(copy)
    total = summed[-1][place].astype(jnp.float32)
    for i, copy in enumerate(outgoing):
        copy.wait_recv()
        total = total + final[i].astype(jnp.float32)
    out_ref[...] = total
    for row in copies:
        for copy in row:
            copy.wait_send()
    for copy in outgoing:
        copy.wait_send()
    if side is not None:
        exchange.wait()


def reduce_pieces(x, halves, last, number, given=None, side=None):
    rows, columns = x.shape[-2:]
    n = last[1]
    stages = len(halves)
    shapes = [(n,) + (2,) * (stages - 1 - s) + (rows, columns) for s in range(stages)]
    vmem = pl.BlockSpec(memory_space=pltpu.VMEM)
    out_shape, in_specs, out_specs = [jax.ShapeDtypeStruct((rows, columns), jnp.float32)], [vmem], [vmem]
    operands, semaphores = [x], []
    if side is not None:
        any_spec = pl.BlockSpec(memory_space=pl.ANY)
        out_shape.append(jax.ShapeDtypeStruct(given.shape[1:], given.dtype))
        in_specs.append(any_spec)
        out_specs.append(any_spec)
        operands.append(given)
        semaphores = [pltpu.SemaphoreType.DMA, pltpu.SemaphoreType.DMA]
    return pl.pallas_call(
        functools.partial(reduce_kernel, tuple(halves), last, side),
        out_shape=tuple(out_shape),
        in_specs=in_specs,
        out_specs=tuple(out_specs),
        scratch_shapes=[pltpu.VMEM(shape, x.dtype) for shape in shapes]
        + [pltpu.VMEM(shape, x.dtype) for shape in shapes]
        + [
            pltpu.VMEM((n - 1, rows, columns), x.dtype),
            pltpu.SemaphoreType.DMA(((stages + 1) * n,)),
            pltpu.SemaphoreType.DMA(((stages + 1) * n,)),
        ]
        + semaphores,
        compiler_params=pltpu.CompilerParams(
            collective_id=number, has_side_effects=True, vmem_limit_bytes=VMEM_BYTES
        ),
    )(*operands)


def swapped(array, axis, step):
    size = lax.axis_size(axis)
    return lax.ppermute(array, axis, [(i, i ^ step) for i in range(size)])


def joined(array, other, place):
    return jnp.where(place == 0, jnp.stack([array, other]), jnp.stack([other, array]))


def by_fsdp(array, dim):
    axis, size, stride = dim
    count = lax.axis_size(axis)
    place = coordinate(dim)
    blocks = [array]
    for k in range(1, size):
        pairs = []
        for i in range(count):
            c = i // stride % size
            pairs.append((i, i + ((c - k) % size - c) * stride))
        blocks.append(lax.ppermute(array, axis, pairs))
    stacked = jnp.stack(blocks)
    order = lax.rem(jnp.arange(size, dtype=jnp.int32) - place + size, size)
    return stacked[order]


def rms_scale(values):
    return lax.rsqrt(jnp.mean(values * values, axis=-1, keepdims=True) + EPSILON)


def rotate(values, places, direction):
    head_count = values.shape[-1] // HEAD_SIZE
    shaped = values.reshape(values.shape[0], head_count, HEAD_SIZE)
    half_dim = HEAD_SIZE // 2
    frequency = 1.0 / 10000.0 ** (jnp.arange(half_dim, dtype=jnp.float32) * 2.0 / HEAD_SIZE)
    angles = places.astype(jnp.float32)[:, None, None] * frequency[None, None, :]
    cosine = jnp.cos(angles)
    sine_table = jnp.sin(angles) * direction
    first_half = shaped[..., :half_dim]
    second_half = shaped[..., half_dim:]
    turned = jnp.concatenate(
        [
            first_half * cosine - second_half * sine_table,
            second_half * cosine + first_half * sine_table,
        ],
        axis=-1,
    )
    return turned.reshape(values.shape)


def local(
    tokens,
    w_query,
    key_projection_weight,
    value_projection_weight,
    w_out,
    w_gate,
    w_up,
    w_down,
    norm_in,
    norm_mid,
    gate_values,
    routes,
    doc_ids,
    cotangent,
):
    local_rows, model_width = tokens.shape
    fsdp = lax.axis_size("fsdp")
    tensor = lax.axis_size("tensor")
    groups = min(fsdp, EXPERTS)
    copies = fsdp // groups
    per_owner = EXPERTS // groups
    piece = local_rows // tensor
    depth = w_gate.shape[1]
    hidden_width = w_gate.shape[2]
    context_index = lax.axis_index("context")
    tensor_index = lax.axis_index("tensor")
    fsdp_all = ("fsdp", fsdp, 1)
    fsdp_dim = ("fsdp", groups, copies)
    context_dim = ("context", lax.axis_size("context"), 1)
    core_dim = ("tensor", 2, 1)
    y_dim = ("tensor", tensor // 2, 2)
    q_width, k_width = w_query.shape[1], key_projection_weight.shape[1]
    columns = per_owner * hidden_width

    def to_owner(weight):
        blocks = jnp.transpose(weight.reshape(groups, per_owner, depth, hidden_width), (0, 2, 1, 3))
        return blocks.reshape(groups, depth, columns)

    packed = jnp.concatenate([to_owner(w_gate), to_owner(w_up), to_owner(w_down)], axis=2)
    packed = jnp.repeat(packed, copies, axis=0)
    cot_piece = lax.dynamic_slice_in_dim(cotangent, tensor_index * piece, piece, 0)
    dense_gates = jnp.sum(
        jnp.where(
            routes.T[None, :, :] == jnp.arange(EXPERTS, dtype=jnp.int32)[:, None, None],
            gate_values.T[None, :, :],
            0.0,
        ),
        axis=1,
    )
    attn_shard = jnp.concatenate(
        [w_query, key_projection_weight, value_projection_weight, w_out], axis=1
    )
    gain_shard = jnp.pad(
        jnp.stack([norm_in, norm_mid]).astype(jnp.float32), ((0, 6), (0, 128 - depth))
    )
    attn_weight, gains = gather_pieces(
        [attn_shard, gain_shard], [[fsdp_all, context_dim]] * 2, 1
    )
    packed, cot_first, dense_gates, attn_weight = lax.optimization_barrier(
        (packed, cot_piece, dense_gates, attn_weight)
    )
    from_fsdp = lax.all_to_all(packed, "fsdp", 0, 0, tiled=True)
    cot_f = by_fsdp(cot_first, fsdp_dim)
    cot_y = by_fsdp(cot_f, y_dim)
    cot_t = by_fsdp(cot_y, core_dim)
    cot_all = jnp.transpose(cot_t, (2, 1, 0, 3, 4)).reshape(-1, model_width)
    gates_all = by_fsdp(dense_gates, fsdp_dim)
    gates_own = lax.dynamic_slice_in_dim(
        gates_all, coordinate(fsdp_dim) * per_owner, per_owner, 1
    )
    gates_rows = jnp.transpose(gates_own, (0, 2, 1)).reshape(-1, per_owner)
    gates_wide = jnp.repeat(gates_rows, hidden_width, axis=1)

    attn_weight = attn_weight.reshape(model_width, -1)
    gains = gains[..., :depth].reshape(-1, 8, depth)
    gain_one = gains[:, 0, :].reshape(-1)
    gain_two = gains[:, 1, :].reshape(-1)
    in_weight = attn_weight[:, : q_width + 2 * k_width]
    out_weight = attn_weight[:, q_width + 2 * k_width :]
    documents = doc_ids[0]
    query_places = context_index * local_rows + jnp.arange(local_rows, dtype=jnp.int32)
    key_places = jnp.arange(documents.shape[0], dtype=jnp.int32)
    score_scale = HEAD_SIZE ** (-0.5)
    inputs = tokens.astype(jnp.float32)
    scale_in = rms_scale(inputs)
    normed_in = (inputs * scale_in * gain_one).astype(jnp.bfloat16)
    projected = jnp.dot(normed_in, in_weight, preferred_element_type=jnp.float32)
    query_input = rotate(projected[:, :q_width], query_places, 1.0).astype(jnp.bfloat16)
    key_local = rotate(projected[:, q_width : q_width + k_width], query_places, 1.0)
    key_value = jnp.concatenate([key_local, projected[:, q_width + k_width :]], axis=1).astype(
        jnp.bfloat16
    )
    key_value = joined(key_value, swapped(key_value, "context", 1), context_index).reshape(
        -1, 2 * k_width
    )
    keys_all, values_all = key_value[:, :k_width], key_value[:, k_width:]
    kv_heads = keys_all.shape[1] // HEAD_SIZE
    per_group = query_input.shape[1] // HEAD_SIZE // kv_heads
    query_head_rows = query_input.reshape(local_rows, kv_heads, per_group, HEAD_SIZE)
    key_head_rows = keys_all.reshape(keys_all.shape[0], kv_heads, HEAD_SIZE)
    value_head_rows = values_all.reshape(values_all.shape[0], kv_heads, HEAD_SIZE)
    visible = (key_places[None, :] <= query_places[:, None]) & (
        documents[None, :] == documents[query_places][:, None]
    )

    def masked_scores():
        raw_scores = (
            jnp.einsum(
                "rkgd,skd->kgrs", query_head_rows, key_head_rows, preferred_element_type=jnp.float32
            )
            * score_scale
        )
        return jnp.where(visible, raw_scores, -1e30)

    masked = masked_scores()
    highest = jnp.max(masked, axis=-1, keepdims=True)
    exponent = jnp.exp(masked - highest)
    totals = jnp.sum(exponent, axis=-1, keepdims=True)
    probs_low = (exponent / totals).astype(jnp.bfloat16)
    context = jnp.einsum(
        "kgrs,skd->rkgd", probs_low, value_head_rows, preferred_element_type=jnp.float32
    )
    context = context.reshape(local_rows, -1).astype(jnp.bfloat16)
    attn_part = lax.dot_general(
        context, out_weight, CONTRACT_COLUMNS, preferred_element_type=jnp.float32
    )
    def by_tensor(part):
        return part.astype(jnp.bfloat16).reshape(tensor // 2, 2, piece, model_width)

    attended = reduce_pieces(by_tensor(attn_part), [core_dim], y_dim, 2)[0]
    start_row = tensor_index * piece
    own_inputs = lax.dynamic_slice_in_dim(tokens, start_row, piece, 0).astype(jnp.float32)
    own_scale_in = lax.dynamic_slice_in_dim(scale_in, start_row, piece, 0)
    hidden_state = own_inputs + attended
    scale_mid = rms_scale(hidden_state)
    normed_mid = (hidden_state * scale_mid * gain_two).astype(jnp.bfloat16)
    expert_rows, both_context = gather_pieces(
        [normed_mid, from_fsdp], [[fsdp_dim, y_dim, core_dim], [context_dim]], 3
    )
    expert_weight = jnp.swapaxes(both_context, 0, 1).reshape(model_width, 3 * columns)
    gate_up_weight = expert_weight[:, : 2 * columns]
    down_weight = expert_weight[:, 2 * columns :]
    expert_rows = expert_rows.reshape(-1, model_width)
    act = jnp.dot(expert_rows, gate_up_weight, preferred_element_type=jnp.float32)
    gate_act, up_act = act[:, :columns], act[:, columns:]
    sigmoid_gate = jax.nn.sigmoid(gate_act)
    swish_act = gate_act * sigmoid_gate
    hidden = (gates_wide * swish_act * up_act).astype(jnp.bfloat16)
    d_hidden = gates_wide * jnp.dot(cot_all, down_weight, preferred_element_type=jnp.float32)
    d_gate_act = d_hidden * up_act * sigmoid_gate * (1.0 + gate_act * (1.0 - sigmoid_gate))
    d_up_act = d_hidden * swish_act
    d_act = jnp.concatenate([d_gate_act, d_up_act], axis=1).astype(jnp.bfloat16)
    moe_part = lax.dot_general(
        hidden, down_weight, CONTRACT_COLUMNS, preferred_element_type=jnp.float32
    ).astype(jnp.bfloat16)
    d_mid_part = lax.dot_general(
        d_act, gate_up_weight, CONTRACT_COLUMNS, preferred_element_type=jnp.float32
    ).astype(jnp.bfloat16)
    split = (groups, tensor // 2, 2, piece, model_width)
    both_parts = jnp.concatenate([moe_part.reshape(split), d_mid_part.reshape(split)], axis=3)
    grad_gate_up = lax.dot_general(
        expert_rows, d_act, CONTRACT_ROWS, preferred_element_type=jnp.float32
    )
    grad_down = lax.dot_general(cot_all, hidden, CONTRACT_ROWS, preferred_element_type=jnp.float32)
    expert_grad = jnp.concatenate([grad_gate_up, grad_down], axis=1).astype(jnp.bfloat16)
    expert_grad = jnp.swapaxes(expert_grad.reshape(fsdp, -1, depth, 3 * columns), 0, 1)
    kept = lax.dynamic_index_in_dim(expert_grad, context_index, 0, False)
    back, taken = reduce_pieces(
        both_parts, [core_dim, y_dim], fsdp_dim, 4, expert_grad, context_dim
    )
    half_grad = (kept.astype(jnp.float32) + taken.astype(jnp.float32)).astype(jnp.bfloat16)
    owned_grad = lax.all_to_all(half_grad, "fsdp", 0, 0, tiled=True).astype(jnp.float32)
    owned_grad = jnp.sum(owned_grad.reshape(groups, copies, depth, 3, per_owner, hidden_width), 1)
    owned_grad = jnp.transpose(owned_grad, (2, 0, 3, 1, 4)).reshape(
        3, EXPERTS, depth, hidden_width
    )

    moe_mixed, d_mid = back[:piece], back[piece:]
    own_output = (hidden_state + moe_mixed).astype(jnp.bfloat16)
    d_gain_mid = jnp.sum(d_mid * hidden_state * scale_mid, axis=0)
    d_hidden_state = (
        cot_piece.astype(jnp.float32)
        + d_mid * gain_two * scale_mid
        - hidden_state
        * scale_mid**3
        * jnp.mean(gain_two * d_mid * hidden_state, axis=-1, keepdims=True)
    )
    d_attended, output = gather_pieces(
        [d_hidden_state.astype(jnp.bfloat16), own_output], [[y_dim, core_dim]] * 2, 5
    )
    d_attended = d_attended.reshape(local_rows, model_width)
    output = output.reshape(local_rows, model_width)
    d_out_weight = lax.dot_general(
        d_attended, context, CONTRACT_ROWS, preferred_element_type=jnp.float32
    )
    d_context = jnp.dot(d_attended, out_weight, preferred_element_type=jnp.float32).astype(
        jnp.bfloat16
    )
    d_context_heads = d_context.reshape(local_rows, kv_heads, per_group, HEAD_SIZE)
    attn_probs = jnp.exp(masked_scores() - highest) / totals
    d_probs = jnp.einsum(
        "rkgd,skd->kgrs", d_context_heads, value_head_rows, preferred_element_type=jnp.float32
    )
    d_scores = attn_probs * (d_probs - jnp.sum(attn_probs * d_probs, axis=-1, keepdims=True))
    d_scores_low = jnp.where(visible, d_scores, 0.0).astype(jnp.bfloat16)
    d_query_turned = jnp.einsum(
        "kgrs,skd->rkgd", d_scores_low, key_head_rows, preferred_element_type=jnp.float32
    )
    d_query_turned = d_query_turned.reshape(local_rows, -1) * score_scale
    d_keys = jnp.einsum(
        "kgrs,rkgd->skd", d_scores_low, query_head_rows, preferred_element_type=jnp.float32
    )
    d_keys = d_keys.reshape(keys_all.shape[0], -1) * score_scale
    d_values = jnp.einsum(
        "kgrs,rkgd->skd", probs_low, d_context_heads, preferred_element_type=jnp.float32
    )
    d_values = d_values.reshape(values_all.shape[0], -1)
    d_both = jnp.concatenate([d_keys, d_values], axis=1).reshape(
        -1, local_rows, 2 * k_width
    )
    d_given = lax.dynamic_index_in_dim(d_both, 1 - context_index, 0, False)
    d_kept = lax.dynamic_index_in_dim(d_both, context_index, 0, False)
    d_own = d_kept + swapped(d_given, "context", 1)
    d_query = rotate(d_query_turned, query_places, -1.0).astype(jnp.bfloat16)
    d_key = rotate(d_own[:, :k_width], query_places, -1.0).astype(jnp.bfloat16)
    d_projected = jnp.concatenate(
        [d_query, d_key, d_own[:, k_width:].astype(jnp.bfloat16)], axis=1
    )
    d_in_part = lax.dot_general(
        d_projected, in_weight, CONTRACT_COLUMNS, preferred_element_type=jnp.float32
    )
    d_in = reduce_pieces(by_tensor(d_in_part), [core_dim], y_dim, 6)[0]
    d_in_weight = lax.dot_general(
        normed_in, d_projected, CONTRACT_ROWS, preferred_element_type=jnp.float32
    )
    d_gain_in = jnp.sum(d_in * own_inputs * own_scale_in, axis=0)
    d_inputs = (
        d_hidden_state
        + d_in * gain_one * own_scale_in
        - own_inputs
        * own_scale_in**3
        * jnp.mean(gain_one * d_in * own_inputs, axis=-1, keepdims=True)
    ).astype(jnp.bfloat16)
    d_gains = jnp.pad(jnp.stack([d_gain_in, d_gain_mid]), ((0, 6), (0, 0)))
    d_tokens, d_gains = gather_pieces([d_inputs, d_gains], [[y_dim, core_dim]] * 2, 7)
    d_tokens = d_tokens.reshape(local_rows, model_width)
    d_gains = jnp.sum(d_gains, axis=(0, 1))[:2]
    d_attn = jnp.concatenate([d_in_weight, d_out_weight], axis=1).astype(jnp.bfloat16)
    d_attn = d_attn.reshape(fsdp, -1, depth, d_attn.shape[1])
    d_gains = jnp.transpose(d_gains.reshape(2, fsdp, -1, depth), (1, 2, 0, 3)).astype(jnp.bfloat16)
    d_gains = jnp.pad(d_gains, ((0, 0), (0, 0), (0, 14), (0, d_attn.shape[3] - depth)))
    owned = reduce_pieces(
        jnp.concatenate([d_attn, d_gains], axis=2), [context_dim], fsdp_all, 8
    )[0]
    first, second = q_width, q_width + k_width
    third = q_width + 2 * k_width
    return (
        output,
        d_tokens,
        owned[:depth, :first],
        owned[:depth, first:second],
        owned[:depth, second:third],
        owned[:depth, third:],
        owned_grad[0],
        owned_grad[1],
        owned_grad[2],
        owned[depth, :depth],
        owned[depth + 1, :depth],
    )


def solution(mesh):
    placed = (
        P(("fsdp", "context"), None),
        P(("fsdp", "context"), "tensor"),
        P(("fsdp", "context"), "tensor"),
        P(("fsdp", "context"), "tensor"),
        P(("fsdp", "context"), "tensor"),
        P(None, ("fsdp", "context"), "tensor"),
        P(None, ("fsdp", "context"), "tensor"),
        P(None, ("fsdp", "context"), "tensor"),
        P(("fsdp", "context")),
        P(("fsdp", "context")),
        P(("fsdp", "context"), None),
        P(("fsdp", "context"), None),
        P("fsdp", None),
        P(("fsdp", "context"), None),
    )
    return jax.shard_map(
        local,
        mesh=mesh,
        in_specs=placed,
        out_specs=(
            P(("fsdp", "context"), None),
            P(("fsdp", "context"), None),
            P(("fsdp", "context"), "tensor"),
            P(("fsdp", "context"), "tensor"),
            P(("fsdp", "context"), "tensor"),
            P(("fsdp", "context"), "tensor"),
            P(None, ("fsdp", "context"), "tensor"),
            P(None, ("fsdp", "context"), "tensor"),
            P(None, ("fsdp", "context"), "tensor"),
            P(("fsdp", "context")),
            P(("fsdp", "context")),
        ),
        check_vma=False,
    )
```

```python
import functools
import math

import jax
import jax.numpy as jnp
from jax import lax
from jax.experimental import pallas as pl
from jax.experimental.pallas import tpu as pltpu
from jax.sharding import PartitionSpec as P

HEAD_SIZE = 64
TOP = 8
EXPERTS = 16

EPSILON = 1e-06
CONTRACT_ROWS = (((0,), (0,)), ((), ()))
CONTRACT_COLUMNS = (((1,), (1,)), ((), ()))
MESH = pl.DeviceIdType.MESH
VMEM_BYTES = 48 * 1024 * 1024


def coordinate(dim):
    axis, size, stride = dim
    return lax.rem(lax.div(lax.axis_index(axis), stride), size)


def device_at(dim, place):
    axis, _, stride = dim
    return {axis: lax.axis_index(axis) + (place - coordinate(dim)) * stride}


def greet(dims):
    barrier = pltpu.get_barrier_semaphore()
    total = 0
    for dim in dims:
        for k in range(1, dim[1]):
            place = lax.rem(coordinate(dim) + k, dim[1])
            pl.semaphore_signal(
                barrier, inc=1, device_id=device_at(dim, place), device_id_type=MESH
            )
            total += 1
    pl.semaphore_wait(barrier, total)


def gather_kernel(jobs, *refs):
    count = len(jobs)
    sources, outs = refs[:count], refs[count : 2 * count]
    send_sem, recv_sem, own_sem = refs[2 * count :]

    def slot(dims, steps):
        return tuple(
            lax.rem(coordinate(dim) - step + dim[1], dim[1]) for step, dim in zip(steps, dims)
        )

    own = []
    for a, dims in enumerate(jobs):
        at = slot(dims, (0,) * len(dims))
        own.append(pltpu.make_async_copy(sources[a], outs[a].at[at], own_sem.at[a]))
    greet(unique(dim for dims in jobs for dim in dims))
    sent = []
    queues = [[] for _ in jobs]

    def forward(a, steps, level, source):
        dims = jobs[a]
        for s in range(level, len(dims)):
            for k in range(1, dims[s][1]):
                index = len(sent)
                copy = pltpu.make_async_remote_copy(
                    src_ref=source,
                    dst_ref=outs[a].at[slot(dims, steps)],
                    send_sem=send_sem.at[index],
                    recv_sem=recv_sem.at[index],
                    device_id=device_at(dims[s], lax.rem(coordinate(dims[s]) + k, dims[s][1])),
                    device_id_type=MESH,
                )
                copy.start()
                sent.append(copy)
                queues[a].append((steps[:s] + (k,) + steps[s + 1 :], s + 1, copy))

    for a, dims in enumerate(jobs):
        forward(a, (0,) * len(dims), 0, sources[a])
    for copy in own:
        copy.start()
    for a, dims in enumerate(jobs):
        at = 0
        while at < len(queues[a]):
            steps, level, copy = queues[a][at]
            at += 1
            copy.wait_recv()
            forward(a, steps, level, outs[a].at[slot(dims, steps)])
    for copy in sent:
        copy.wait_send()
    for copy in own:
        copy.wait()


def unique(dims):
    kept = []
    for dim in dims:
        if dim not in kept:
            kept.append(dim)
    return kept


def gather_pieces(arrays, jobs, number):
    shapes, copies = [], 0
    for a, dims in zip(arrays, jobs):
        sizes = tuple(dim[1] for dim in dims)
        shapes.append(jax.ShapeDtypeStruct(sizes + a.shape, a.dtype))
        copies += math.prod(sizes) - 1
    any_spec = pl.BlockSpec(memory_space=pl.ANY)
    return pl.pallas_call(
        functools.partial(gather_kernel, jobs),
        out_shape=tuple(shapes),
        in_specs=[any_spec] * len(arrays),
        out_specs=tuple(any_spec for _ in arrays),
        scratch_shapes=[
            pltpu.SemaphoreType.DMA((copies,)),
            pltpu.SemaphoreType.DMA((copies,)),
            pltpu.SemaphoreType.DMA((len(arrays),)),
        ],
        cost_estimate=pl.CostEstimate(flops=0, bytes_accessed=60_000_000, transcendentals=0),
        compiler_params=pltpu.CompilerParams(collective_id=number, has_side_effects=True),
    )(*arrays)


def reduce_kernel(halves, last, side, *refs):
    if side is None:
        x_ref, out_ref, *scratch = refs
    else:
        x_ref, given_ref, out_ref, taken_ref, *scratch, side_send, side_recv = refs
    stages = len(halves)
    landed = scratch[:stages]
    summed = scratch[stages : 2 * stages]
    final = scratch[2 * stages]
    send_sem, recv_sem = scratch[2 * stages + 1 :]
    n = last[1]
    place = coordinate(last)
    mine = [coordinate(dim) for dim in halves]
    greet(list(halves) + [last] + ([] if side is None else [side]))
    order = [lax.rem(place + k, n) for k in list(range(1, n)) + [0]]

    def held(stage):
        return x_ref if stage == 0 else summed[stage - 1]

    def part(stage, j, which):
        return (j,) + (slice(None),) * (stages - 1 - stage) + (which,)

    copies = [[None] * n for _ in range(stages)]

    def push(stage, i):
        copies[stage][i] = pltpu.make_async_remote_copy(
            src_ref=held(stage).at[part(stage, order[i], 1 - mine[stage])],
            dst_ref=landed[stage].at[i],
            send_sem=send_sem.at[stage * n + i],
            recv_sem=recv_sem.at[stage * n + i],
            device_id=device_at(halves[stage], 1 - mine[stage]),
            device_id_type=MESH,
        )
        copies[stage][i].start()

    def merge(stage, i):
        copies[stage][i].wait_recv()
        kept = held(stage)[part(stage, order[i], mine[stage])]
        both = kept.astype(jnp.float32) + landed[stage][i].astype(jnp.float32)
        summed[stage][order[i]] = both.astype(summed[stage].dtype)

    for i in range(n):
        push(0, i)
    if side is not None:
        exchange = pltpu.make_async_remote_copy(
            src_ref=given_ref.at[1],
            dst_ref=taken_ref,
            send_sem=side_send,
            recv_sem=side_recv,
            device_id=device_at(side, 1 - coordinate(side)),
            device_id_type=MESH,
        )
        exchange.start()
    outgoing = []
    for tick in range(n + stages - 1):
        for stage in range(stages):
            i = tick - stage
            if 0 <= i < n:
                merge(stage, i)
                if stage + 1 < stages:
                    push(stage + 1, i)
                elif i < n - 1:
                    index = stages * n + i
                    copy = pltpu.make_async_remote_copy(
                        src_ref=summed[-1].at[order[i]],
                        dst_ref=final.at[i],
                        send_sem=send_sem.at[index],
                        recv_sem=recv_sem.at[index],
                        device_id=device_at(last, order[i]),
                        device_id_type=MESH,
                    )
                    copy.start()
                    outgoing.append(copy)
    total = summed[-1][place].astype(jnp.float32)
    for i, copy in enumerate(outgoing):
        copy.wait_recv()
        total = total + final[i].astype(jnp.float32)
    out_ref[...] = total
    for row in copies:
        for copy in row:
            copy.wait_send()
    for copy in outgoing:
        copy.wait_send()
    if side is not None:
        exchange.wait()


def reduce_pieces(x, halves, last, number, given=None, side=None):
    rows, columns = x.shape[-2:]
    n = last[1]
    stages = len(halves)
    shapes = [(n,) + (2,) * (stages - 1 - s) + (rows, columns) for s in range(stages)]
    vmem = pl.BlockSpec(memory_space=pltpu.VMEM)
    out_shape, in_specs, out_specs = [jax.ShapeDtypeStruct((rows, columns), jnp.float32)], [vmem], [vmem]
    operands, semaphores = [x], []
    if side is not None:
        any_spec = pl.BlockSpec(memory_space=pl.ANY)
        out_shape.append(jax.ShapeDtypeStruct(given.shape[1:], given.dtype))
        in_specs.append(any_spec)
        out_specs.append(any_spec)
        operands.append(given)
        semaphores = [pltpu.SemaphoreType.DMA, pltpu.SemaphoreType.DMA]
    return pl.pallas_call(
        functools.partial(reduce_kernel, tuple(halves), last, side),
        out_shape=tuple(out_shape),
        in_specs=in_specs,
        out_specs=tuple(out_specs),
        scratch_shapes=[pltpu.VMEM(shape, x.dtype) for shape in shapes]
        + [pltpu.VMEM(shape, x.dtype) for shape in shapes]
        + [
            pltpu.VMEM((n - 1, rows, columns), x.dtype),
            pltpu.SemaphoreType.DMA(((stages + 1) * n,)),
            pltpu.SemaphoreType.DMA(((stages + 1) * n,)),
        ]
        + semaphores,
        cost_estimate=pl.CostEstimate(flops=0, bytes_accessed=60_000_000, transcendentals=0),
        compiler_params=pltpu.CompilerParams(
            collective_id=number, has_side_effects=True, vmem_limit_bytes=VMEM_BYTES
        ),
    )(*operands)


def swapped(array, axis, step):
    size = lax.axis_size(axis)
    return lax.ppermute(array, axis, [(i, i ^ step) for i in range(size)])


def joined(array, other, place):
    return jnp.where(place == 0, jnp.stack([array, other]), jnp.stack([other, array]))


def own_first(rows, place, depth):
    parts = jnp.swapaxes(rows.reshape(rows.shape[0], -1, 2, depth), 1, 2)
    return jnp.where(place == 0, parts, parts[:, ::-1]).reshape(rows.shape)


def in_order(rows, place, depth):
    parts = rows.reshape(rows.shape[0], 2, -1, depth)
    parts = jnp.where(place == 0, parts, parts[:, ::-1])
    return jnp.swapaxes(parts, 1, 2).reshape(rows.shape)


def rms_scale(values):
    return lax.rsqrt(jnp.mean(values * values, axis=-1, keepdims=True) + EPSILON)


def rotate(values, places, direction):
    head_count = values.shape[-1] // HEAD_SIZE
    shaped = values.reshape(values.shape[0], head_count, HEAD_SIZE)
    half_dim = HEAD_SIZE // 2
    frequency = 1.0 / 10000.0 ** (jnp.arange(half_dim, dtype=jnp.float32) * 2.0 / HEAD_SIZE)
    angles = places.astype(jnp.float32)[:, None, None] * frequency[None, None, :]
    cosine = jnp.cos(angles)
    sine_table = jnp.sin(angles) * direction
    first_half = shaped[..., :half_dim]
    second_half = shaped[..., half_dim:]
    turned = jnp.concatenate(
        [
            first_half * cosine - second_half * sine_table,
            second_half * cosine + first_half * sine_table,
        ],
        axis=-1,
    )
    return turned.reshape(values.shape)


def local(
    tokens,
    w_query,
    key_projection_weight,
    value_projection_weight,
    w_out,
    w_gate,
    w_up,
    w_down,
    norm_in,
    norm_mid,
    gate_values,
    routes,
    doc_ids,
    cotangent,
):
    local_rows, model_width = tokens.shape
    fsdp = lax.axis_size("fsdp")
    tensor = lax.axis_size("tensor")
    groups = min(fsdp, EXPERTS)
    copies = fsdp // groups
    per_owner = EXPERTS // groups
    piece = local_rows // tensor
    depth = w_gate.shape[1]
    hidden_width = w_gate.shape[2]
    context_index = lax.axis_index("context")
    tensor_index = lax.axis_index("tensor")
    fsdp_all = ("fsdp", fsdp, 1)
    fsdp_dim = ("fsdp", groups, copies)
    context_dim = ("context", lax.axis_size("context"), 1)
    core_dim = ("tensor", 2, 1)
    y_dim = ("tensor", tensor // 2, 2)
    q_width, k_width = w_query.shape[1], key_projection_weight.shape[1]
    columns = per_owner * hidden_width

    def to_owner(weight):
        blocks = jnp.transpose(weight.reshape(groups, per_owner, depth, hidden_width), (0, 2, 1, 3))
        return blocks.reshape(groups, depth, columns)

    packed = jnp.concatenate([to_owner(w_gate), to_owner(w_up), to_owner(w_down)], axis=2)
    packed = jnp.repeat(packed, copies, axis=0)
    cot_piece = lax.dynamic_slice_in_dim(cotangent, tensor_index * piece, piece, 0)
    dense_gates = jnp.sum(
        jnp.where(
            routes.T[None, :, :] == jnp.arange(EXPERTS, dtype=jnp.int32)[:, None, None],
            gate_values.T[None, :, :],
            0.0,
        ),
        axis=1,
    )
    attn_shard = jnp.concatenate(
        [w_query, key_projection_weight, value_projection_weight, w_out], axis=1
    )
    gain_shard = jnp.pad(
        jnp.stack([norm_in, norm_mid]).astype(jnp.float32), ((0, 6), (0, 128 - depth))
    )
    attn_weight, gains, gates_all, cot_all = gather_pieces(
        [attn_shard, gain_shard, dense_gates, own_first(cot_piece, context_index, depth)],
        [[fsdp_all, context_dim]] * 2 + [[fsdp_dim], [fsdp_dim, y_dim, core_dim]],
        1,
    )
    cot_all = cot_all.reshape(-1, model_width)
    packed, attn_weight = lax.optimization_barrier((packed, attn_weight))
    from_fsdp = lax.all_to_all(packed, "fsdp", 0, 0, tiled=True)
    gates_own = lax.dynamic_slice_in_dim(
        gates_all, coordinate(fsdp_dim) * per_owner, per_owner, 1
    )
    gates_rows = jnp.transpose(gates_own, (0, 2, 1)).reshape(-1, per_owner)
    gates_wide = jnp.repeat(gates_rows, hidden_width, axis=1)
    attn_weight = attn_weight.reshape(model_width, -1)
    gains = gains[..., :depth].reshape(-1, 8, depth)
    gain_one = gains[:, 0, :].reshape(-1)
    gain_two = gains[:, 1, :].reshape(-1)
    in_weight = attn_weight[:, : q_width + 2 * k_width]
    out_weight = attn_weight[:, q_width + 2 * k_width :]
    documents = doc_ids[0]
    query_places = context_index * local_rows + jnp.arange(local_rows, dtype=jnp.int32)
    key_places = jnp.arange(documents.shape[0], dtype=jnp.int32)
    score_scale = HEAD_SIZE ** (-0.5)
    inputs = tokens.astype(jnp.float32)
    scale_in = rms_scale(inputs)
    normed_in = (inputs * scale_in * gain_one).astype(jnp.bfloat16)
    projected = jnp.dot(normed_in, in_weight, preferred_element_type=jnp.float32)
    query_input = rotate(projected[:, :q_width], query_places, 1.0).astype(jnp.bfloat16)
    key_local = rotate(projected[:, q_width : q_width + k_width], query_places, 1.0)
    key_value = jnp.concatenate([key_local, projected[:, q_width + k_width :]], axis=1).astype(
        jnp.bfloat16
    )
    key_value = joined(key_value, swapped(key_value, "context", 1), context_index).reshape(
        -1, 2 * k_width
    )
    keys_all, values_all = key_value[:, :k_width], key_value[:, k_width:]
    kv_heads = keys_all.shape[1] // HEAD_SIZE
    per_group = query_input.shape[1] // HEAD_SIZE // kv_heads
    query_head_rows = query_input.reshape(local_rows, kv_heads, per_group, HEAD_SIZE)
    key_head_rows = keys_all.reshape(keys_all.shape[0], kv_heads, HEAD_SIZE)
    value_head_rows = values_all.reshape(values_all.shape[0], kv_heads, HEAD_SIZE)
    visible = (key_places[None, :] <= query_places[:, None]) & (
        documents[None, :] == documents[query_places][:, None]
    )

    def masked_scores():
        raw_scores = (
            jnp.einsum(
                "rkgd,skd->kgrs", query_head_rows, key_head_rows, preferred_element_type=jnp.float32
            )
            * score_scale
        )
        return jnp.where(visible, raw_scores, -1e30)

    masked = masked_scores()
    highest = jnp.max(masked, axis=-1, keepdims=True)
    exponent = jnp.exp(masked - highest)
    totals = jnp.sum(exponent, axis=-1, keepdims=True)
    probs_low = (exponent / totals).astype(jnp.bfloat16)
    context = jnp.einsum(
        "kgrs,skd->rkgd", probs_low, value_head_rows, preferred_element_type=jnp.float32
    )
    context = context.reshape(local_rows, -1).astype(jnp.bfloat16)
    attn_part = lax.dot_general(
        context, out_weight, CONTRACT_COLUMNS, preferred_element_type=jnp.float32
    )
    def by_tensor(part):
        return part.astype(jnp.bfloat16).reshape(tensor // 2, 2, piece, model_width)

    attn_part, from_fsdp = lax.optimization_barrier((attn_part, from_fsdp))
    from_context = swapped(from_fsdp, "context", 1)
    attended = reduce_pieces(by_tensor(attn_part), [core_dim], y_dim, 2)[0]
    start_row = tensor_index * piece
    own_inputs = lax.dynamic_slice_in_dim(tokens, start_row, piece, 0).astype(jnp.float32)
    own_scale_in = lax.dynamic_slice_in_dim(scale_in, start_row, piece, 0)
    hidden_state = own_inputs + attended
    scale_mid = rms_scale(hidden_state)
    normed_mid = (hidden_state * scale_mid * gain_two).astype(jnp.bfloat16)
    (expert_rows,) = gather_pieces(
        [own_first(normed_mid, context_index, depth)], [[fsdp_dim, y_dim, core_dim]], 3
    )
    expert_weight = jnp.concatenate([from_fsdp, from_context]).reshape(model_width, 3 * columns)
    gate_up_weight = expert_weight[:, : 2 * columns]
    down_weight = expert_weight[:, 2 * columns :]
    expert_rows = expert_rows.reshape(-1, model_width)
    act = jnp.dot(expert_rows, gate_up_weight, preferred_element_type=jnp.float32)
    gate_act, up_act = act[:, :columns], act[:, columns:]
    sigmoid_gate = jax.nn.sigmoid(gate_act)
    swish_act = gate_act * sigmoid_gate
    hidden = (gates_wide * swish_act * up_act).astype(jnp.bfloat16)
    d_hidden = gates_wide * jnp.dot(cot_all, down_weight, preferred_element_type=jnp.float32)
    d_gate_act = d_hidden * up_act * sigmoid_gate * (1.0 + gate_act * (1.0 - sigmoid_gate))
    d_up_act = d_hidden * swish_act
    d_act = jnp.concatenate([d_gate_act, d_up_act], axis=1).astype(jnp.bfloat16)
    moe_part = lax.dot_general(
        hidden, down_weight, CONTRACT_COLUMNS, preferred_element_type=jnp.float32
    ).astype(jnp.bfloat16)
    d_mid_part = lax.dot_general(
        d_act, gate_up_weight, CONTRACT_COLUMNS, preferred_element_type=jnp.float32
    ).astype(jnp.bfloat16)
    split = (groups, tensor // 2, 2, piece, model_width)
    both_parts = jnp.concatenate([moe_part.reshape(split), d_mid_part.reshape(split)], axis=3)
    grad_gate_up = lax.dot_general(
        expert_rows, d_act, CONTRACT_ROWS, preferred_element_type=jnp.float32
    )
    grad_down = lax.dot_general(cot_all, hidden, CONTRACT_ROWS, preferred_element_type=jnp.float32)
    expert_grad = jnp.concatenate([grad_gate_up, grad_down], axis=1).astype(jnp.bfloat16)
    expert_grad = expert_grad.reshape(2, fsdp, depth, 3 * columns)
    kept = expert_grad[0]
    back, taken = reduce_pieces(
        both_parts, [core_dim, y_dim], fsdp_dim, 4, expert_grad, context_dim
    )
    half_grad = (kept.astype(jnp.float32) + taken.astype(jnp.float32)).astype(jnp.bfloat16)
    owned_grad = lax.all_to_all(half_grad, "fsdp", 0, 0, tiled=True).astype(jnp.float32)
    owned_grad = jnp.sum(owned_grad.reshape(groups, copies, depth, 3, per_owner, hidden_width), 1)
    owned_grad = jnp.transpose(owned_grad, (2, 0, 3, 1, 4)).reshape(
        3, EXPERTS, depth, hidden_width
    )

    back = in_order(back, context_index, depth)
    moe_mixed, d_mid = back[:piece], back[piece:]
    own_output = (hidden_state + moe_mixed).astype(jnp.bfloat16)
    d_gain_mid = jnp.sum(d_mid * hidden_state * scale_mid, axis=0)
    d_hidden_state = (
        cot_piece.astype(jnp.float32)
        + d_mid * gain_two * scale_mid
        - hidden_state
        * scale_mid**3
        * jnp.mean(gain_two * d_mid * hidden_state, axis=-1, keepdims=True)
    )
    d_attended, output = gather_pieces(
        [d_hidden_state.astype(jnp.bfloat16), own_output], [[y_dim, core_dim]] * 2, 5
    )
    d_attended = d_attended.reshape(local_rows, model_width)
    output = output.reshape(local_rows, model_width)
    d_out_weight = lax.dot_general(
        d_attended, context, CONTRACT_ROWS, preferred_element_type=jnp.float32
    )
    d_context = jnp.dot(d_attended, out_weight, preferred_element_type=jnp.float32).astype(
        jnp.bfloat16
    )
    d_context_heads = d_context.reshape(local_rows, kv_heads, per_group, HEAD_SIZE)
    attn_probs = jnp.exp(masked_scores() - highest) / totals
    d_probs = jnp.einsum(
        "rkgd,skd->kgrs", d_context_heads, value_head_rows, preferred_element_type=jnp.float32
    )
    d_scores = attn_probs * (d_probs - jnp.sum(attn_probs * d_probs, axis=-1, keepdims=True))
    d_scores_low = jnp.where(visible, d_scores, 0.0).astype(jnp.bfloat16)
    d_query_turned = jnp.einsum(
        "kgrs,skd->rkgd", d_scores_low, key_head_rows, preferred_element_type=jnp.float32
    )
    d_query_turned = d_query_turned.reshape(local_rows, -1) * score_scale
    d_keys = jnp.einsum(
        "kgrs,rkgd->skd", d_scores_low, query_head_rows, preferred_element_type=jnp.float32
    )
    d_keys = d_keys.reshape(keys_all.shape[0], -1) * score_scale
    d_values = jnp.einsum(
        "kgrs,rkgd->skd", probs_low, d_context_heads, preferred_element_type=jnp.float32
    )
    d_values = d_values.reshape(values_all.shape[0], -1)
    d_both = jnp.concatenate([d_keys, d_values], axis=1).reshape(
        -1, local_rows, 2 * k_width
    )
    d_given = lax.dynamic_index_in_dim(d_both, 1 - context_index, 0, False)
    d_kept = lax.dynamic_index_in_dim(d_both, context_index, 0, False)
    d_own = d_kept + swapped(d_given, "context", 1)
    d_query = rotate(d_query_turned, query_places, -1.0).astype(jnp.bfloat16)
    d_key = rotate(d_own[:, :k_width], query_places, -1.0).astype(jnp.bfloat16)
    d_projected = jnp.concatenate(
        [d_query, d_key, d_own[:, k_width:].astype(jnp.bfloat16)], axis=1
    )
    d_in_part = lax.dot_general(
        d_projected, in_weight, CONTRACT_COLUMNS, preferred_element_type=jnp.float32
    )
    d_in = reduce_pieces(by_tensor(d_in_part), [core_dim], y_dim, 6)[0]
    d_in_weight = lax.dot_general(
        normed_in, d_projected, CONTRACT_ROWS, preferred_element_type=jnp.float32
    )
    d_gain_in = jnp.sum(d_in * own_inputs * own_scale_in, axis=0)
    d_inputs = (
        d_hidden_state
        + d_in * gain_one * own_scale_in
        - own_inputs
        * own_scale_in**3
        * jnp.mean(gain_one * d_in * own_inputs, axis=-1, keepdims=True)
    ).astype(jnp.bfloat16)
    d_gains = jnp.pad(jnp.stack([d_gain_in, d_gain_mid]), ((0, 6), (0, 0)))
    d_tokens, d_gains = gather_pieces([d_inputs, d_gains], [[y_dim, core_dim]] * 2, 7)
    d_tokens = d_tokens.reshape(local_rows, model_width)
    d_gains = jnp.sum(d_gains, axis=(0, 1))[:2]
    d_attn = jnp.concatenate([d_in_weight, d_out_weight], axis=1).astype(jnp.bfloat16)
    d_attn = d_attn.reshape(fsdp, -1, depth, d_attn.shape[1])
    d_gains = jnp.transpose(d_gains.reshape(2, fsdp, -1, depth), (1, 2, 0, 3)).astype(jnp.bfloat16)
    d_gains = jnp.pad(d_gains, ((0, 0), (0, 0), (0, 14), (0, d_attn.shape[3] - depth)))
    owned = reduce_pieces(
        jnp.concatenate([d_attn, d_gains], axis=2), [context_dim], fsdp_all, 8
    )[0]
    first, second = q_width, q_width + k_width
    third = q_width + 2 * k_width
    return (
        output,
        d_tokens,
        owned[:depth, :first],
        owned[:depth, first:second],
        owned[:depth, second:third],
        owned[:depth, third:],
        owned_grad[0],
        owned_grad[1],
        owned_grad[2],
        owned[depth, :depth],
        owned[depth + 1, :depth],
    )


def solution(mesh):
    placed = (
        P(("fsdp", "context"), None),
        P(("fsdp", "context"), "tensor"),
        P(("fsdp", "context"), "tensor"),
        P(("fsdp", "context"), "tensor"),
        P(("fsdp", "context"), "tensor"),
        P(None, ("fsdp", "context"), "tensor"),
        P(None, ("fsdp", "context"), "tensor"),
        P(None, ("fsdp", "context"), "tensor"),
        P(("fsdp", "context")),
        P(("fsdp", "context")),
        P(("fsdp", "context"), None),
        P(("fsdp", "context"), None),
        P("fsdp", None),
        P(("fsdp", "context"), None),
    )
    return jax.shard_map(
        local,
        mesh=mesh,
        in_specs=placed,
        out_specs=(
            P(("fsdp", "context"), None),
            P(("fsdp", "context"), None),
            P(("fsdp", "context"), "tensor"),
            P(("fsdp", "context"), "tensor"),
            P(("fsdp", "context"), "tensor"),
            P(("fsdp", "context"), "tensor"),
            P(None, ("fsdp", "context"), "tensor"),
            P(None, ("fsdp", "context"), "tensor"),
            P(None, ("fsdp", "context"), "tensor"),
            P(("fsdp", "context")),
            P(("fsdp", "context")),
        ),
        check_vma=False,
    )
```

```python
import functools
import math

import jax
import jax.numpy as jnp
from jax import lax
from jax.experimental import pallas as pl
from jax.experimental.pallas import tpu as pltpu
from jax.sharding import PartitionSpec as P

HEAD_SIZE = 64
TOP = 8
EXPERTS = 16

EPSILON = 1e-06
CONTRACT_ROWS = (((0,), (0,)), ((), ()))
CONTRACT_COLUMNS = (((1,), (1,)), ((), ()))
MESH = pl.DeviceIdType.MESH
VMEM_BYTES = 48 * 1024 * 1024


def coordinate(dim):
    axis, size, stride = dim
    return lax.rem(lax.div(lax.axis_index(axis), stride), size)


def device_at(dim, place):
    axis, _, stride = dim
    return {axis: lax.axis_index(axis) + (place - coordinate(dim)) * stride}


def greet(dims):
    barrier = pltpu.get_barrier_semaphore()
    total = 0
    for dim in dims:
        for k in range(1, dim[1]):
            place = lax.rem(coordinate(dim) + k, dim[1])
            pl.semaphore_signal(
                barrier, inc=1, device_id=device_at(dim, place), device_id_type=MESH
            )
            total += 1
    pl.semaphore_wait(barrier, total)


def gather_kernel(jobs, *refs):
    count = len(jobs)
    sources, outs = refs[:count], refs[count : 2 * count]
    send_sem, recv_sem, own_sem = refs[2 * count :]

    def slot(dims, steps):
        return tuple(
            lax.rem(coordinate(dim) - step + dim[1], dim[1]) for step, dim in zip(steps, dims)
        )

    own = []
    for a, dims in enumerate(jobs):
        at = slot(dims, (0,) * len(dims))
        own.append(pltpu.make_async_copy(sources[a], outs[a].at[at], own_sem.at[a]))
    greet(unique(dim for dims in jobs for dim in dims))
    sent = []
    queues = [[] for _ in jobs]

    def forward(a, steps, level, source):
        dims = jobs[a]
        for s in range(level, len(dims)):
            for k in range(1, dims[s][1]):
                index = len(sent)
                copy = pltpu.make_async_remote_copy(
                    src_ref=source,
                    dst_ref=outs[a].at[slot(dims, steps)],
                    send_sem=send_sem.at[index],
                    recv_sem=recv_sem.at[index],
                    device_id=device_at(dims[s], lax.rem(coordinate(dims[s]) + k, dims[s][1])),
                    device_id_type=MESH,
                )
                copy.start()
                sent.append(copy)
                queues[a].append((steps[:s] + (k,) + steps[s + 1 :], s + 1, copy))

    for a, dims in enumerate(jobs):
        forward(a, (0,) * len(dims), 0, sources[a])
    for copy in own:
        copy.start()
    for a, dims in enumerate(jobs):
        at = 0
        while at < len(queues[a]):
            steps, level, copy = queues[a][at]
            at += 1
            copy.wait_recv()
            forward(a, steps, level, outs[a].at[slot(dims, steps)])
    for copy in sent:
        copy.wait_send()
    for copy in own:
        copy.wait()


def unique(dims):
    kept = []
    for dim in dims:
        if dim not in kept:
            kept.append(dim)
    return kept


def gather_pieces(arrays, jobs, number):
    shapes, copies = [], 0
    for a, dims in zip(arrays, jobs):
        sizes = tuple(dim[1] for dim in dims)
        shapes.append(jax.ShapeDtypeStruct(sizes + a.shape, a.dtype))
        copies += math.prod(sizes) - 1
    any_spec = pl.BlockSpec(memory_space=pl.ANY)
    return pl.pallas_call(
        functools.partial(gather_kernel, jobs),
        out_shape=tuple(shapes),
        in_specs=[any_spec] * len(arrays),
        out_specs=tuple(any_spec for _ in arrays),
        scratch_shapes=[
            pltpu.SemaphoreType.DMA((copies,)),
            pltpu.SemaphoreType.DMA((copies,)),
            pltpu.SemaphoreType.DMA((len(arrays),)),
        ],
        cost_estimate=pl.CostEstimate(flops=0, bytes_accessed=60_000_000, transcendentals=0),
        compiler_params=pltpu.CompilerParams(collective_id=number, has_side_effects=True),
    )(*arrays)


def reduce_kernel(halves, last, side, *refs):
    if side is None:
        x_ref, out_ref, *scratch = refs
    else:
        x_ref, given_ref, out_ref, taken_ref, *scratch, side_send, side_recv = refs
    stages = len(halves)
    landed = scratch[:stages]
    summed = scratch[stages : 2 * stages]
    final = scratch[2 * stages]
    send_sem, recv_sem = scratch[2 * stages + 1 :]
    n = last[1]
    place = coordinate(last)
    mine = [coordinate(dim) for dim in halves]
    greet(list(halves) + [last] + ([] if side is None else [side]))
    order = [lax.rem(place + k, n) for k in list(range(1, n)) + [0]]

    def held(stage):
        return x_ref if stage == 0 else summed[stage - 1]

    def part(stage, j, which):
        return (j,) + (slice(None),) * (stages - 1 - stage) + (which,)

    copies = [[None] * n for _ in range(stages)]

    def push(stage, i):
        copies[stage][i] = pltpu.make_async_remote_copy(
            src_ref=held(stage).at[part(stage, order[i], 1 - mine[stage])],
            dst_ref=landed[stage].at[i],
            send_sem=send_sem.at[stage * n + i],
            recv_sem=recv_sem.at[stage * n + i],
            device_id=device_at(halves[stage], 1 - mine[stage]),
            device_id_type=MESH,
        )
        copies[stage][i].start()

    def merge(stage, i):
        copies[stage][i].wait_recv()
        kept = held(stage)[part(stage, order[i], mine[stage])]
        both = kept.astype(jnp.float32) + landed[stage][i].astype(jnp.float32)
        summed[stage][order[i]] = both.astype(summed[stage].dtype)

    for i in range(n):
        push(0, i)
    if side is not None:
        exchange = pltpu.make_async_remote_copy(
            src_ref=given_ref.at[1],
            dst_ref=taken_ref,
            send_sem=side_send,
            recv_sem=side_recv,
            device_id=device_at(side, 1 - coordinate(side)),
            device_id_type=MESH,
        )
        exchange.start()
    outgoing = []
    for tick in range(n + stages - 1):
        for stage in range(stages):
            i = tick - stage
            if 0 <= i < n:
                merge(stage, i)
                if stage + 1 < stages:
                    push(stage + 1, i)
                elif i < n - 1:
                    index = stages * n + i
                    copy = pltpu.make_async_remote_copy(
                        src_ref=summed[-1].at[order[i]],
                        dst_ref=final.at[i],
                        send_sem=send_sem.at[index],
                        recv_sem=recv_sem.at[index],
                        device_id=device_at(last, order[i]),
                        device_id_type=MESH,
                    )
                    copy.start()
                    outgoing.append(copy)
    total = summed[-1][place].astype(jnp.float32)
    for i, copy in enumerate(outgoing):
        copy.wait_recv()
        total = total + final[i].astype(jnp.float32)
    out_ref[...] = total
    for row in copies:
        for copy in row:
            copy.wait_send()
    for copy in outgoing:
        copy.wait_send()
    if side is not None:
        exchange.wait()


def reduce_pieces(x, halves, last, number, given=None, side=None):
    rows, columns = x.shape[-2:]
    n = last[1]
    stages = len(halves)
    shapes = [(n,) + (2,) * (stages - 1 - s) + (rows, columns) for s in range(stages)]
    vmem = pl.BlockSpec(memory_space=pltpu.VMEM)
    out_shape, in_specs, out_specs = [jax.ShapeDtypeStruct((rows, columns), jnp.float32)], [vmem], [vmem]
    operands, semaphores = [x], []
    if side is not None:
        any_spec = pl.BlockSpec(memory_space=pl.ANY)
        out_shape.append(jax.ShapeDtypeStruct(given.shape[1:], given.dtype))
        in_specs.append(any_spec)
        out_specs.append(any_spec)
        operands.append(given)
        semaphores = [pltpu.SemaphoreType.DMA, pltpu.SemaphoreType.DMA]
    return pl.pallas_call(
        functools.partial(reduce_kernel, tuple(halves), last, side),
        out_shape=tuple(out_shape),
        in_specs=in_specs,
        out_specs=tuple(out_specs),
        scratch_shapes=[pltpu.VMEM(shape, x.dtype) for shape in shapes]
        + [pltpu.VMEM(shape, x.dtype) for shape in shapes]
        + [
            pltpu.VMEM((n - 1, rows, columns), x.dtype),
            pltpu.SemaphoreType.DMA(((stages + 1) * n,)),
            pltpu.SemaphoreType.DMA(((stages + 1) * n,)),
        ]
        + semaphores,
        cost_estimate=pl.CostEstimate(flops=0, bytes_accessed=60_000_000, transcendentals=0),
        compiler_params=pltpu.CompilerParams(
            collective_id=number, has_side_effects=True, vmem_limit_bytes=VMEM_BYTES
        ),
    )(*operands)


def swapped(array, axis, step):
    size = lax.axis_size(axis)
    return lax.ppermute(array, axis, [(i, i ^ step) for i in range(size)])


def joined(array, other, place):
    return jnp.where(place == 0, jnp.stack([array, other]), jnp.stack([other, array]))


def own_first(rows, place, depth):
    parts = jnp.swapaxes(rows.reshape(rows.shape[0], -1, 2, depth), 1, 2)
    return jnp.where(place == 0, parts, parts[:, ::-1]).reshape(rows.shape)


def in_order(rows, place, depth):
    parts = rows.reshape(rows.shape[0], 2, -1, depth)
    parts = jnp.where(place == 0, parts, parts[:, ::-1])
    return jnp.swapaxes(parts, 1, 2).reshape(rows.shape)


def rms_scale(values):
    return lax.rsqrt(jnp.mean(values * values, axis=-1, keepdims=True) + EPSILON)


def rotate(values, places, direction):
    head_count = values.shape[-1] // HEAD_SIZE
    shaped = values.reshape(values.shape[0], head_count, HEAD_SIZE)
    half_dim = HEAD_SIZE // 2
    frequency = 1.0 / 10000.0 ** (jnp.arange(half_dim, dtype=jnp.float32) * 2.0 / HEAD_SIZE)
    angles = places.astype(jnp.float32)[:, None, None] * frequency[None, None, :]
    cosine = jnp.cos(angles)
    sine_table = jnp.sin(angles) * direction
    first_half = shaped[..., :half_dim]
    second_half = shaped[..., half_dim:]
    turned = jnp.concatenate(
        [
            first_half * cosine - second_half * sine_table,
            second_half * cosine + first_half * sine_table,
        ],
        axis=-1,
    )
    return turned.reshape(values.shape)


def local(
    tokens,
    w_query,
    key_projection_weight,
    value_projection_weight,
    w_out,
    w_gate,
    w_up,
    w_down,
    norm_in,
    norm_mid,
    gate_values,
    routes,
    doc_ids,
    cotangent,
):
    local_rows, model_width = tokens.shape
    fsdp = lax.axis_size("fsdp")
    tensor = lax.axis_size("tensor")
    groups = min(fsdp, EXPERTS)
    copies = fsdp // groups
    per_owner = EXPERTS // groups
    piece = local_rows // tensor
    depth = w_gate.shape[1]
    hidden_width = w_gate.shape[2]
    context_index = lax.axis_index("context")
    tensor_index = lax.axis_index("tensor")
    fsdp_all = ("fsdp", fsdp, 1)
    fsdp_dim = ("fsdp", groups, copies)
    context_dim = ("context", lax.axis_size("context"), 1)
    core_dim = ("tensor", 2, 1)
    y_dim = ("tensor", tensor // 2, 2)
    q_width, k_width = w_query.shape[1], key_projection_weight.shape[1]
    columns = per_owner * hidden_width

    def to_owner(weight):
        blocks = jnp.transpose(weight.reshape(groups, per_owner, depth, hidden_width), (0, 2, 1, 3))
        return blocks.reshape(groups, depth, columns)

    packed = jnp.concatenate([to_owner(w_gate), to_owner(w_up), to_owner(w_down)], axis=2)
    packed = jnp.repeat(packed, copies, axis=0)
    cot_piece = lax.dynamic_slice_in_dim(cotangent, tensor_index * piece, piece, 0)
    dense_gates = jnp.sum(
        jnp.where(
            routes.T[None, :, :] == jnp.arange(EXPERTS, dtype=jnp.int32)[:, None, None],
            gate_values.T[None, :, :],
            0.0,
        ),
        axis=1,
    )
    attn_shard = jnp.concatenate(
        [w_query, key_projection_weight, value_projection_weight, w_out], axis=1
    )
    gain_shard = jnp.pad(
        jnp.stack([norm_in, norm_mid]).astype(jnp.float32), ((0, 6), (0, 128 - depth))
    )
    attn_weight, gains, gates_all, cot_all = gather_pieces(
        [attn_shard, gain_shard, dense_gates, own_first(cot_piece, context_index, depth)],
        [[fsdp_all, context_dim]] * 2 + [[fsdp_dim], [fsdp_dim, y_dim, core_dim]],
        1,
    )
    cot_all = cot_all.reshape(-1, model_width)
    packed, attn_weight = lax.optimization_barrier((packed, attn_weight))
    from_fsdp = lax.all_to_all(packed, "fsdp", 0, 0, tiled=True)
    gates_own = lax.dynamic_slice_in_dim(
        gates_all, coordinate(fsdp_dim) * per_owner, per_owner, 1
    )
    gates_rows = jnp.transpose(gates_own, (0, 2, 1)).reshape(-1, per_owner)
    gates_wide = jnp.repeat(gates_rows, hidden_width, axis=1)
    attn_weight = attn_weight.reshape(model_width, -1)
    gains = gains[..., :depth].reshape(-1, 8, depth)
    gain_one = gains[:, 0, :].reshape(-1)
    gain_two = gains[:, 1, :].reshape(-1)
    in_weight = attn_weight[:, : q_width + 2 * k_width]
    out_weight = attn_weight[:, q_width + 2 * k_width :]
    documents = doc_ids[0]
    query_places = context_index * local_rows + jnp.arange(local_rows, dtype=jnp.int32)
    key_places = jnp.arange(documents.shape[0], dtype=jnp.int32)
    score_scale = HEAD_SIZE ** (-0.5)
    inputs = tokens.astype(jnp.float32)
    scale_in = rms_scale(inputs)
    normed_in = (inputs * scale_in * gain_one).astype(jnp.bfloat16)
    projected = jnp.dot(normed_in, in_weight, preferred_element_type=jnp.float32)
    query_input = rotate(projected[:, :q_width], query_places, 1.0).astype(jnp.bfloat16)
    key_local = rotate(projected[:, q_width : q_width + k_width], query_places, 1.0)
    key_value = jnp.concatenate([key_local, projected[:, q_width + k_width :]], axis=1).astype(
        jnp.bfloat16
    )
    key_value = joined(key_value, swapped(key_value, "context", 1), context_index).reshape(
        -1, 2 * k_width
    )
    keys_all, values_all = key_value[:, :k_width], key_value[:, k_width:]
    kv_heads = keys_all.shape[1] // HEAD_SIZE
    per_group = query_input.shape[1] // HEAD_SIZE // kv_heads
    query_head_rows = query_input.reshape(local_rows, kv_heads, per_group, HEAD_SIZE)
    key_head_rows = keys_all.reshape(keys_all.shape[0], kv_heads, HEAD_SIZE)
    value_head_rows = values_all.reshape(values_all.shape[0], kv_heads, HEAD_SIZE)
    visible = (key_places[None, :] <= query_places[:, None]) & (
        documents[None, :] == documents[query_places][:, None]
    )

    def masked_scores():
        raw_scores = (
            jnp.einsum(
                "rkgd,skd->kgrs", query_head_rows, key_head_rows, preferred_element_type=jnp.float32
            )
            * score_scale
        )
        return jnp.where(visible, raw_scores, -1e30)

    masked = masked_scores()
    highest = jnp.max(masked, axis=-1, keepdims=True)
    exponent = jnp.exp(masked - highest)
    totals = jnp.sum(exponent, axis=-1, keepdims=True)
    probs_low = (exponent / totals).astype(jnp.bfloat16)
    context = jnp.einsum(
        "kgrs,skd->rkgd", probs_low, value_head_rows, preferred_element_type=jnp.float32
    )
    context = context.reshape(local_rows, -1).astype(jnp.bfloat16)
    attn_part = lax.dot_general(
        context, out_weight, CONTRACT_COLUMNS, preferred_element_type=jnp.float32
    )
    def by_tensor(part):
        return part.astype(jnp.bfloat16).reshape(tensor // 2, 2, piece, model_width)

    attn_part, from_fsdp = lax.optimization_barrier((attn_part, from_fsdp))
    from_context = swapped(from_fsdp, "context", 1)
    attended = reduce_pieces(by_tensor(attn_part), [core_dim], y_dim, 2)[0]
    start_row = tensor_index * piece
    own_inputs = lax.dynamic_slice_in_dim(tokens, start_row, piece, 0).astype(jnp.float32)
    own_scale_in = lax.dynamic_slice_in_dim(scale_in, start_row, piece, 0)
    hidden_state = own_inputs + attended
    scale_mid = rms_scale(hidden_state)
    normed_mid = (hidden_state * scale_mid * gain_two).astype(jnp.bfloat16)
    (expert_rows,) = gather_pieces(
        [own_first(normed_mid, context_index, depth)], [[fsdp_dim, y_dim, core_dim]], 3
    )
    expert_weight = jnp.concatenate([from_fsdp, from_context]).reshape(model_width, 3 * columns)
    gate_up_weight = expert_weight[:, : 2 * columns]
    down_weight = expert_weight[:, 2 * columns :]
    expert_rows = expert_rows.reshape(-1, model_width)
    act = jnp.dot(expert_rows, gate_up_weight, preferred_element_type=jnp.float32)
    gate_act, up_act = act[:, :columns], act[:, columns:]
    sigmoid_gate = jax.nn.sigmoid(gate_act)
    swish_act = gate_act * sigmoid_gate
    hidden = (gates_wide * swish_act * up_act).astype(jnp.bfloat16)
    d_hidden = gates_wide * jnp.dot(cot_all, down_weight, preferred_element_type=jnp.float32)
    d_gate_act = d_hidden * up_act * sigmoid_gate * (1.0 + gate_act * (1.0 - sigmoid_gate))
    d_up_act = d_hidden * swish_act
    d_act = jnp.concatenate([d_gate_act, d_up_act], axis=1).astype(jnp.bfloat16)
    moe_part = lax.dot_general(
        hidden, down_weight, CONTRACT_COLUMNS, preferred_element_type=jnp.float32
    ).astype(jnp.bfloat16)
    d_mid_part = lax.dot_general(
        d_act, gate_up_weight, CONTRACT_COLUMNS, preferred_element_type=jnp.float32
    ).astype(jnp.bfloat16)
    split = (groups, tensor // 2, 2, piece, model_width)
    both_parts = jnp.concatenate([moe_part.reshape(split), d_mid_part.reshape(split)], axis=3)
    grad_gate_up = lax.dot_general(
        expert_rows, d_act, CONTRACT_ROWS, preferred_element_type=jnp.float32
    )
    grad_down = lax.dot_general(cot_all, hidden, CONTRACT_ROWS, preferred_element_type=jnp.float32)
    expert_grad = jnp.concatenate([grad_gate_up, grad_down], axis=1).astype(jnp.bfloat16)
    expert_grad = expert_grad.reshape(2, fsdp, depth, 3 * columns)
    kept = expert_grad[0]
    back, taken = reduce_pieces(
        both_parts, [core_dim, y_dim], fsdp_dim, 4, expert_grad, context_dim
    )
    half_grad = (kept.astype(jnp.float32) + taken.astype(jnp.float32)).astype(jnp.bfloat16)
    back = in_order(back, context_index, depth)
    moe_mixed, d_mid = back[:piece], back[piece:]
    own_output = (hidden_state + moe_mixed).astype(jnp.bfloat16)
    d_gain_mid = jnp.sum(d_mid * hidden_state * scale_mid, axis=0)
    d_hidden_state = (
        cot_piece.astype(jnp.float32)
        + d_mid * gain_two * scale_mid
        - hidden_state
        * scale_mid**3
        * jnp.mean(gain_two * d_mid * hidden_state, axis=-1, keepdims=True)
    )
    own_attended, half_grad = lax.optimization_barrier(
        (d_hidden_state.astype(jnp.bfloat16), half_grad)
    )
    owned_grad = lax.all_to_all(half_grad, "fsdp", 0, 0, tiled=True).astype(jnp.float32)
    owned_grad = jnp.sum(owned_grad.reshape(groups, copies, depth, 3, per_owner, hidden_width), 1)
    owned_grad = jnp.transpose(owned_grad, (2, 0, 3, 1, 4)).reshape(
        3, EXPERTS, depth, hidden_width
    )
    d_attended, output = gather_pieces(
        [own_attended, own_output], [[y_dim, core_dim]] * 2, 5
    )
    d_attended = d_attended.reshape(local_rows, model_width)
    output = output.reshape(local_rows, model_width)
    d_out_weight = lax.dot_general(
        d_attended, context, CONTRACT_ROWS, preferred_element_type=jnp.float32
    )
    d_context = jnp.dot(d_attended, out_weight, preferred_element_type=jnp.float32).astype(
        jnp.bfloat16
    )
    d_context_heads = d_context.reshape(local_rows, kv_heads, per_group, HEAD_SIZE)
    attn_probs = jnp.exp(masked_scores() - highest) / totals
    d_probs = jnp.einsum(
        "rkgd,skd->kgrs", d_context_heads, value_head_rows, preferred_element_type=jnp.float32
    )
    d_scores = attn_probs * (d_probs - jnp.sum(attn_probs * d_probs, axis=-1, keepdims=True))
    d_scores_low = jnp.where(visible, d_scores, 0.0).astype(jnp.bfloat16)
    d_query_turned = jnp.einsum(
        "kgrs,skd->rkgd", d_scores_low, key_head_rows, preferred_element_type=jnp.float32
    )
    d_query_turned = d_query_turned.reshape(local_rows, -1) * score_scale
    d_keys = jnp.einsum(
        "kgrs,rkgd->skd", d_scores_low, query_head_rows, preferred_element_type=jnp.float32
    )
    d_keys = d_keys.reshape(keys_all.shape[0], -1) * score_scale
    d_values = jnp.einsum(
        "kgrs,rkgd->skd", probs_low, d_context_heads, preferred_element_type=jnp.float32
    )
    d_values = d_values.reshape(values_all.shape[0], -1)
    d_both = jnp.concatenate([d_keys, d_values], axis=1).reshape(
        -1, local_rows, 2 * k_width
    )
    d_given = lax.dynamic_index_in_dim(d_both, 1 - context_index, 0, False)
    d_kept = lax.dynamic_index_in_dim(d_both, context_index, 0, False)
    d_own = d_kept + swapped(d_given, "context", 1)
    d_query = rotate(d_query_turned, query_places, -1.0).astype(jnp.bfloat16)
    d_key = rotate(d_own[:, :k_width], query_places, -1.0).astype(jnp.bfloat16)
    d_projected = jnp.concatenate(
        [d_query, d_key, d_own[:, k_width:].astype(jnp.bfloat16)], axis=1
    )
    d_in_part = lax.dot_general(
        d_projected, in_weight, CONTRACT_COLUMNS, preferred_element_type=jnp.float32
    )
    d_in = reduce_pieces(by_tensor(d_in_part), [core_dim], y_dim, 6)[0]
    d_in_weight = lax.dot_general(
        normed_in, d_projected, CONTRACT_ROWS, preferred_element_type=jnp.float32
    )
    d_gain_in = jnp.sum(d_in * own_inputs * own_scale_in, axis=0)
    d_inputs = (
        d_hidden_state
        + d_in * gain_one * own_scale_in
        - own_inputs
        * own_scale_in**3
        * jnp.mean(gain_one * d_in * own_inputs, axis=-1, keepdims=True)
    ).astype(jnp.bfloat16)
    d_gains = jnp.pad(jnp.stack([d_gain_in, d_gain_mid]), ((0, 6), (0, 0)))
    d_tokens, d_gains = gather_pieces([d_inputs, d_gains], [[y_dim, core_dim]] * 2, 7)
    d_tokens = d_tokens.reshape(local_rows, model_width)
    d_gains = jnp.sum(d_gains, axis=(0, 1))[:2]
    d_attn = jnp.concatenate([d_in_weight, d_out_weight], axis=1).astype(jnp.bfloat16)
    d_attn = d_attn.reshape(fsdp, -1, depth, d_attn.shape[1])
    d_gains = jnp.transpose(d_gains.reshape(2, fsdp, -1, depth), (1, 2, 0, 3)).astype(jnp.bfloat16)
    d_gains = jnp.pad(d_gains, ((0, 0), (0, 0), (0, 14), (0, d_attn.shape[3] - depth)))
    owned = reduce_pieces(
        jnp.concatenate([d_attn, d_gains], axis=2), [context_dim], fsdp_all, 8
    )[0]
    first, second = q_width, q_width + k_width
    third = q_width + 2 * k_width
    return (
        output,
        d_tokens,
        owned[:depth, :first],
        owned[:depth, first:second],
        owned[:depth, second:third],
        owned[:depth, third:],
        owned_grad[0],
        owned_grad[1],
        owned_grad[2],
        owned[depth, :depth],
        owned[depth + 1, :depth],
    )


def solution(mesh):
    placed = (
        P(("fsdp", "context"), None),
        P(("fsdp", "context"), "tensor"),
        P(("fsdp", "context"), "tensor"),
        P(("fsdp", "context"), "tensor"),
        P(("fsdp", "context"), "tensor"),
        P(None, ("fsdp", "context"), "tensor"),
        P(None, ("fsdp", "context"), "tensor"),
        P(None, ("fsdp", "context"), "tensor"),
        P(("fsdp", "context")),
        P(("fsdp", "context")),
        P(("fsdp", "context"), None),
        P(("fsdp", "context"), None),
        P("fsdp", None),
        P(("fsdp", "context"), None),
    )
    return jax.shard_map(
        local,
        mesh=mesh,
        in_specs=placed,
        out_specs=(
            P(("fsdp", "context"), None),
            P(("fsdp", "context"), None),
            P(("fsdp", "context"), "tensor"),
            P(("fsdp", "context"), "tensor"),
            P(("fsdp", "context"), "tensor"),
            P(("fsdp", "context"), "tensor"),
            P(None, ("fsdp", "context"), "tensor"),
            P(None, ("fsdp", "context"), "tensor"),
            P(None, ("fsdp", "context"), "tensor"),
            P(("fsdp", "context")),
            P(("fsdp", "context")),
        ),
        check_vma=False,
    )
```
